32 devices in a mesh: freq: 4 (over z), tm: 2 (over x), bl: 4 (over y, core).
Axes of the slice: x: 2, y: 2, z: 4, core: 2. Of those that a mesh axis runs over, the one named last changes fastest.
Arguments:
- samples: int32 [1024, 128, 2048], P(('freq', 'bl'), 'tm'), may hold values from 0 to 15
- chan_index: int32 [8], replicated, may hold values from 0 to 1023, as said below
Outputs:
- visibilities: float32 [8, 4, 2, 512, 512], P(('freq', 'tm'), 'bl')
The draws below stay inside these ranges and needn't reach their ends.
Inputs may be any that keep to these rules, and one draw needn't show every extreme that they name: `chan_index`: the entries are distinct.
All inputs are finite; a program needn't handle non-finite values.
Results may differ from the reference program's by a relative error of at most 0.0064.
Values may be sent and summed in bfloat16 or wider, within the bound.
No kernel may reach another device: no remote copies, remote signals or barrier semaphores. Data moves between devices by JAX's collectives and lax.ppermute only.
A program may use at most 192 MiB of HBM per device.

```python
import math
import jax
import jax.numpy as jnp
from jax import lax

NIN = 1024
FRAME = 2048
TAPS = 4
CH = 8
FRAMES = 128


def draw_chan_index(key, part):
    half = FRAME // 2
    inner = jax.random.permutation(key, half - 2)[:CH - 2] + 1
    chosen = jnp.concatenate([inner.astype(jnp.int32), jnp.array([0, half - 1], jnp.int32)])
    order = jax.random.permutation(jax.random.fold_in(key, 7), CH)
    return chosen[order].astype(jnp.int32)


def place_ends(values, key, least, high):
    shape = values.shape
    spot = [jax.random.randint(jax.random.fold_in(key, axis), (), 0, shape[axis]) for axis in range(len(shape))]
    values = values.at[tuple(spot)].set(least)
    longest = shape.index(max(shape))
    spot[longest] = (spot[longest] + 1) % shape[longest]
    return values.at[tuple(spot)].set(high)


def setup_inputs(seed: int = 0) -> dict:
    streams_of = jax.random.split(jax.random.key(seed), 3)
    samples = place_ends(jax.random.randint(streams_of[0], (NIN, FRAMES, FRAME), 0, 16), jax.random.fold_in(streams_of[0], 1), 0, 15).astype(jnp.int32)
    chan_index = draw_chan_index(jax.random.fold_in(streams_of[2], 71), 0)
    return dict(samples=samples, chan_index=chan_index)


def tap_table(frame):
    place = jnp.arange(TAPS * frame, dtype=jnp.float32) + 0.5
    shifted = (place - 2.0 * frame) / frame
    window = 0.5 - 0.5 * jnp.cos(place * (2.0 * math.pi / (TAPS * frame)))
    return (jnp.sinc(shifted) * window).reshape(TAPS, frame)

def dft_table(chan_index, frame):
    steps = jnp.arange(frame, dtype=jnp.int32)
    phase = chan_index[None, :] * steps[:, None] % frame
    angle = phase.astype(jnp.float32) * (2.0 * math.pi / frame)
    scale = 1.0 / math.sqrt(frame)
    both = jnp.stack([jnp.cos(angle) * scale, -jnp.sin(angle) * scale], axis=-1)
    return both.reshape(frame, -1).astype(jnp.bfloat16)

def apply_taps(padded, taps):
    count = padded.shape[1] - (TAPS - 1)
    total = taps[0][None, None, :] * padded[:, 0:count]
    for k in range(1, TAPS):
        total = total + taps[k][None, None, :] * padded[:, k:k + count]
    return total

def reference(samples, chan_index):
    frame = FRAME
    taps = tap_table(frame)
    table = dft_table(chan_index, frame).astype(jnp.float32)
    blocks = samples.reshape(NIN // 16, 16, FRAMES, frame)

    def channelize(block):
        volts = (block.astype(jnp.float32) - 7.5) * 0.25
        zeros = jnp.zeros((16, TAPS - 1, frame), jnp.float32)
        padded = jnp.concatenate([zeros, volts], axis=1)
        filtered = apply_taps(padded, taps).astype(jnp.bfloat16)
        flat = filtered.reshape(16 * FRAMES, frame).astype(jnp.float32)
        spec = jnp.dot(flat, table, preferred_element_type=jnp.float32)
        return spec.astype(jnp.bfloat16).reshape(16, FRAMES, 2 * CH)
    spectra = lax.map(channelize, blocks).reshape(NIN, FRAMES, CH, 2)
    per_chan = jnp.transpose(spectra, (2, 3, 0, 1))
    half = NIN // 2

    def correlate(chan):
        real_part = chan[0].astype(jnp.float32)
        imag_part = chan[1].astype(jnp.float32)
        tiles = []
        for tile in range(4):
            row_block = tile // 2
            col_block = tile % 2
            rows_re = real_part[row_block * half:(row_block + 1) * half]
            rows_im = imag_part[row_block * half:(row_block + 1) * half]
            cols_re = real_part[col_block * half:(col_block + 1) * half]
            cols_im = imag_part[col_block * half:(col_block + 1) * half]
            right = jnp.concatenate([cols_re, cols_im], axis=1)
            left_re = jnp.concatenate([rows_re, rows_im], axis=1)
            left_im = jnp.concatenate([rows_im, -rows_re], axis=1)
            vis_re = jnp.dot(left_re, right.T, preferred_element_type=jnp.float32)
            vis_im = jnp.dot(left_im, right.T, preferred_element_type=jnp.float32)
            tiles.append(jnp.stack([vis_re, vis_im], axis=0) / FRAMES)
        return jnp.stack(tiles, axis=0)
    return lax.map(correlate, per_chan)
```

```python
import functools
import math

import jax
import jax.numpy as jnp
from jax import lax
from jax.experimental import pallas as pl
from jax.experimental.pallas import tpu as pltpu
from jax.sharding import PartitionSpec as P

TAPS = 4
LANES = 128
GROUP = 4


def tap_table(frame):
    place = jnp.arange(TAPS * frame, dtype=jnp.float32) + 0.5
    shifted = (place - 2.0 * frame) / frame
    window = 0.5 - 0.5 * jnp.cos(place * (2.0 * math.pi / (TAPS * frame)))
    return (jnp.sinc(shifted) * window).reshape(TAPS, frame)


def weights(chan_index, frame):
    steps = jnp.arange(frame, dtype=jnp.int32)
    phase = chan_index[:, None] * steps[None, :] % frame
    angle = phase.astype(jnp.float32) * (2.0 * math.pi / frame)
    scale = 1.0 / math.sqrt(frame)
    table = jnp.stack([jnp.cos(angle) * scale, -jnp.sin(angle) * scale])
    table = table.astype(jnp.bfloat16).astype(jnp.float32)
    full = (tap_table(frame)[:, None, None, :] * 0.25 * table[None]).reshape(-1, frame)
    high = full.astype(jnp.bfloat16)
    low = (full - high.astype(jnp.float32)).astype(jnp.bfloat16)
    return jnp.concatenate([high, low], axis=0)


def channelize_kernel(chans, in_dev, fr_dev, w_ref, x_ref, o_ref, spec, carry):
    step = pl.program_id(0)
    frame = x_ref.shape[-1]

    @pl.when(step == 0)
    def _():
        carry[...] = jnp.zeros_like(carry)

    x = (x_ref[...].astype(jnp.float32) - 7.5).astype(jnp.bfloat16).reshape(-1, frame)
    both = lax.dot_general(
        w_ref[...], x, (((1,), (1,)), ((), ())), preferred_element_type=jnp.float32
    )
    half = both.shape[0] // 2
    both = both[:half] + both[half:]
    rows = 2 * chans
    lane = lax.broadcasted_iota(jnp.int32, (rows, LANES), 1)
    place = lane % fr_dev
    first = lax.broadcasted_iota(jnp.int32, (chans, LANES), 1) < fr_dev
    for pair in range(GROUP // 2):
        part = both[:, pair * LANES : (pair + 1) * LANES]
        own = part[(TAPS - 1) * rows :]
        over = jnp.zeros_like(own)
        for k in range(TAPS - 1):
            late = TAPS - 1 - k
            moved = pltpu.roll(part[k * rows : (k + 1) * rows], late, 1)
            own = own + jnp.where(place >= late, moved, 0.0)
            over = over + jnp.where(place < late, moved, 0.0)
        re, im = own[:chans], own[chans:]
        even = jnp.where(first, re, pltpu.roll(im, fr_dev, 1))
        odd = jnp.where(first, pltpu.roll(re, fr_dev, 1), im)
        i = step * GROUP + pair * 2
        spec[pl.ds(i, chans, stride=in_dev), :] = even
        spec[pl.ds(i + 1, chans, stride=in_dev), :] = odd
        shift = (step * (GROUP // 2) + pair) * TAPS
        from_even = jnp.where(lane >= fr_dev, over, 0.0)
        from_odd = jnp.where(lane < fr_dev, over, 0.0)
        carry[0] += pltpu.roll(from_even, (shift + fr_dev) % LANES, 1)
        carry[1] += pltpu.roll(from_odd, shift, 1)

    @pl.when(step == pl.num_programs(0) - 1)
    def _():
        extra = o_ref.shape[1] - in_dev - 4
        for c in range(chans):
            block = [spec[c * in_dev : (c + 1) * in_dev]]
            for p in range(2):
                for odd_one in range(2):
                    block.append(carry[odd_one, p * chans + c : p * chans + c + 1])
            if extra:
                block.append(jnp.zeros((extra, LANES), jnp.float32))
            o_ref[c] = jnp.concatenate(block, axis=0).astype(jnp.bfloat16)


def channelize(samples, table):
    in_dev, fr_dev, frame = samples.shape
    chans = table.shape[0] // (2 * TAPS * 2)
    rows = (in_dev + 4 + 15) // 16 * 16
    return pl.pallas_call(
        functools.partial(channelize_kernel, chans, in_dev, fr_dev),
        grid=(in_dev // GROUP,),
        in_specs=[
            pl.BlockSpec(table.shape, lambda i: (0, 0)),
            pl.BlockSpec((GROUP, fr_dev, frame), lambda i: (i, 0, 0)),
        ],
        out_specs=pl.BlockSpec((chans, rows, LANES), lambda i: (0, 0, 0)),
        out_shape=jax.ShapeDtypeStruct((chans, rows, LANES), jnp.bfloat16),
        scratch_shapes=[
            pltpu.VMEM((chans * in_dev, LANES), jnp.float32),
            pltpu.VMEM((2, 2 * chans, LANES), jnp.float32),
        ],
        compiler_params=pltpu.CompilerParams(vmem_limit_bytes=40 * 2**20),
        name="channelize",
    )(table, samples)


def carry_maps(in_dev, fr_dev):
    mine = lax.broadcasted_iota(jnp.int32, (in_dev, LANES), 0)
    lane = lax.broadcasted_iota(jnp.int32, (in_dev, LANES), 1)
    mask = (lane // TAPS == mine // 2)
    odd = mine % 2 == 1
    src = lax.broadcasted_iota(jnp.int32, (2 * LANES, LANES), 0)
    dst = lax.broadcasted_iota(jnp.int32, (2 * LANES, LANES), 1)
    place = (src // LANES) * fr_dev + src % TAPS
    spread = jnp.where((place == dst) & (src % TAPS < TAPS - 1), 1.0, 0.0).astype(jnp.bfloat16)
    return mask, odd, spread


def with_carry(block, carried, maps):
    mask, odd, spread = maps
    picked = []
    for p in range(2):
        row = jnp.where(odd, carried[2 * p + 1][None], carried[2 * p][None])
        picked.append(jnp.where(mask, row, 0.0).astype(jnp.bfloat16))
    moved = jnp.dot(
        jnp.concatenate(picked, axis=1), spread, preferred_element_type=jnp.float32
    )
    return (block.astype(jnp.float32) + moved).astype(jnp.bfloat16)


def correlate_kernel(n_freq, n_tm, in_dev, fr_dev, scale, where_ref, g_ref, o_ref, left, right):
    n_bl = g_ref.shape[0]
    step = pl.program_id(0)
    per_half = n_freq // 2 * n_bl

    @pl.when(step == 0)
    def _():
        maps = carry_maps(in_dev, fr_dev)
        for out, side in ((left, 0), (right, 1)):
            base = where_ref[side] * (n_freq // 2)
            for m in range(per_half):
                f, b = base + m // n_bl, m % n_bl
                for t in range(n_tm):
                    block = g_ref[b, f * n_tm + t, :in_dev, :]
                    if t:
                        carried = g_ref[b, f * n_tm + t - 1, in_dev : in_dev + 4, :]
                        block = with_carry(block, carried.astype(jnp.float32), maps)
                    out[m * in_dev : (m + 1) * in_dev, t * LANES : (t + 1) * LANES] = block

    rows = o_ref.shape[3]
    mine = left[pl.ds(pl.multiple_of(step * rows, rows), rows), :]
    lane = lax.broadcasted_iota(jnp.int32, (rows, LANES), 1)
    turned = []
    for t in range(n_tm):
        part = mine[:, t * LANES : (t + 1) * LANES].astype(jnp.float32)
        part = pltpu.roll(part, fr_dev, 1)
        turned.append(jnp.where(lane < fr_dev, part, -part).astype(jnp.bfloat16))
    dims = (((1,), (1,)), ((), ()))
    for p, a in enumerate((mine, jnp.concatenate(turned, axis=1))):
        o_ref[0, 0, p] = scale * lax.dot_general(
            a, right[...], dims, preferred_element_type=jnp.float32
        )


def correlate(gathered, where, n_freq, n_tm, in_dev, fr_dev):
    n_bl = gathered.shape[0]
    half = n_freq * n_bl * in_dev // 2
    rows = half // 4
    scale = 1.0 / (n_tm * fr_dev)
    return pl.pallas_call(
        functools.partial(correlate_kernel, n_freq, n_tm, in_dev, fr_dev, scale),
        grid_spec=pltpu.PrefetchScalarGridSpec(
            num_scalar_prefetch=1,
            grid=(half // rows,),
            in_specs=[pl.BlockSpec(gathered.shape, lambda i, w: (0, 0, 0, 0))],
            out_specs=pl.BlockSpec((1, 1, 2, rows, half), lambda i, w: (0, 0, 0, i, 0)),
            scratch_shapes=[pltpu.VMEM((half, n_tm * LANES), jnp.bfloat16)] * 2,
        ),
        out_shape=jax.ShapeDtypeStruct((1, 1, 2, half, half), jnp.float32),
        compiler_params=pltpu.CompilerParams(vmem_limit_bytes=40 * 2**20),
        name="correlate",
    )(where, gathered)


def correlate_plain(gathered, where, n_freq, n_tm, in_dev, fr_dev):
    n_bl = gathered.shape[0]
    half = n_freq * n_bl * in_dev // 2
    blocks = gathered.reshape(n_bl, n_freq, n_tm, -1, LANES)
    blocks = jnp.transpose(blocks, (1, 0, 2, 3, 4)).astype(jnp.float32)
    main = blocks[:, :, :, :in_dev].reshape(n_freq, n_bl, n_tm, in_dev, 2, fr_dev)
    over = blocks[:, :, :-1, in_dev : in_dev + 4, : in_dev // 2 * TAPS]
    over = over.reshape(n_freq, n_bl, n_tm - 1, 2, 2, in_dev // 2, TAPS)
    over = jnp.transpose(over, (0, 1, 2, 5, 4, 3, 6))
    over = over.reshape(n_freq, n_bl, n_tm - 1, in_dev, 2, TAPS)[..., : TAPS - 1]
    over = jnp.pad(over, [(0, 0)] * 2 + [(1, 0)] + [(0, 0)] * 2 + [(0, fr_dev - TAPS + 1)])
    whole = (main + over).astype(jnp.bfloat16)
    whole = jnp.transpose(whole, (4, 0, 1, 3, 2, 5)).reshape(2, 2 * half, n_tm * fr_dev)
    rows = lax.dynamic_slice_in_dim(whole, where[0] * half, half, 1)
    cols = lax.dynamic_slice_in_dim(whole, where[1] * half, half, 1)
    right = jnp.concatenate([cols[0], cols[1]], axis=1)
    left = jnp.stack(
        [jnp.concatenate([rows[0], rows[1]], 1), jnp.concatenate([rows[1], -rows[0]], 1)]
    )
    product = jnp.einsum("phf,qf->phq", left, right, preferred_element_type=jnp.float32)
    return (product / (n_tm * fr_dev))[None, None]


def on_device(samples, chan_index):
    in_dev, fr_dev, frame = samples.shape
    n_freq = lax.axis_size("freq")
    n_tm = lax.axis_size("tm")
    table = weights(chan_index, frame)
    spectra = channelize(samples, table)
    moved = lax.all_to_all(spectra, ("freq", "tm"), split_axis=0, concat_axis=0, tiled=True)
    gathered = lax.all_gather(moved, "bl", axis=0, tiled=False)
    tile = lax.axis_index("bl")
    where = jnp.stack([tile // 2, tile % 2]).astype(jnp.int32)
    form = correlate if in_dev % 16 == 0 else correlate_plain
    return form(gathered, where, n_freq, n_tm, in_dev, fr_dev)


def solution(mesh):
    placed = (P(("freq", "bl"), "tm", None), P())
    return jax.shard_map(
        on_device,
        mesh=mesh,
        in_specs=placed,
        out_specs=P(("freq", "tm"), "bl", None, None, None),
        check_vma=False,
    )
```

```python
import functools
import math

import jax
import jax.numpy as jnp
from jax import lax
from jax.experimental import pallas as pl
from jax.experimental.pallas import tpu as pltpu
from jax.sharding import PartitionSpec as P

TAPS = 4
LANES = 128
GROUP = 4
PARTS = 4


def bin_column(chan_ref, chans):
    row = lax.broadcasted_iota(jnp.int32, (chans, LANES), 0)
    out = jnp.zeros((chans, LANES), jnp.int32)
    for c in range(chans):
        out = jnp.where(row == c, chan_ref[c], out)
    return out[:, :1]


def build_weights(chan_ref, w_ref, chans):
    frame = w_ref.shape[1]
    half = w_ref.shape[0] // 2
    bins = bin_column(chan_ref, chans)
    steps = lax.broadcasted_iota(jnp.int32, (chans, frame), 1)
    angle = (bins * steps % frame).astype(jnp.float32) * (2.0 * math.pi / frame)
    scale = 1.0 / math.sqrt(frame)
    table = jnp.concatenate([jnp.cos(angle) * scale, -jnp.sin(angle) * scale], axis=0)
    table = table.astype(jnp.bfloat16).astype(jnp.float32) * 0.25
    tap = lax.broadcasted_iota(jnp.int32, (8, frame), 0) % TAPS
    place = lax.broadcasted_iota(jnp.int32, (8, frame), 1) + tap * frame
    place = place.astype(jnp.float32) + 0.5
    turn = math.pi * ((place - 2.0 * frame) / frame)
    window = 0.5 - 0.5 * jnp.cos(place * (2.0 * math.pi / (TAPS * frame)))
    taps = jnp.sin(turn) / turn * window
    rows = 2 * chans
    for k in range(TAPS):
        full = taps[k : k + 1] * table
        high = full.astype(jnp.bfloat16)
        low = (full - high.astype(jnp.float32)).astype(jnp.bfloat16)
        w_ref[k * rows : (k + 1) * rows] = high
        w_ref[half + k * rows : half + (k + 1) * rows] = low


def shift_and_add(chans, in_dev, fr_dev, pair, raw, spec, carry):
    rows = 2 * chans
    lane = lax.broadcasted_iota(jnp.int32, (rows, LANES), 1)
    place = lane % fr_dev
    first = lax.broadcasted_iota(jnp.int32, (chans, LANES), 1) < fr_dev
    span = slice(pair * LANES, (pair + 1) * LANES)
    own = raw[(TAPS - 1) * rows :, span]
    over = jnp.zeros_like(own)
    for k in range(TAPS - 1):
        late = TAPS - 1 - k
        moved = pltpu.roll(raw[k * rows : (k + 1) * rows, span], late, 1)
        own = own + jnp.where(place >= late, moved, 0.0)
        over = over + jnp.where(place < late, moved, 0.0)
    re, im = own[:chans], own[chans:]
    even = jnp.where(first, re, pltpu.roll(im, fr_dev, 1))
    odd = jnp.where(first, pltpu.roll(re, fr_dev, 1), im)
    spec[pl.ds(pair * 2, chans, stride=in_dev), :] = even
    spec[pl.ds(pair * 2 + 1, chans, stride=in_dev), :] = odd
    shift = pair * TAPS
    from_even = jnp.where(lane >= fr_dev, over, 0.0)
    from_odd = jnp.where(lane < fr_dev, over, 0.0)
    carry[0] += pltpu.roll(from_even, (shift + fr_dev) % LANES, 1)
    carry[1] += pltpu.roll(from_odd, shift, 1) if shift else from_odd


def channelize_kernel(chans, chan_ref, x_ref, o_ref, buf, w_ref, raw, spec, carry, sems):
    in_dev, fr_dev, frame = x_ref.shape
    count = in_dev // GROUP

    def fetch(g):
        span = pl.ds(g * GROUP, GROUP)
        return pltpu.make_async_copy(x_ref.at[span], buf.at[span], sems.at[g])

    for g in range(count):
        fetch(g).start()
    build_weights(chan_ref, w_ref, chans)
    carry[...] = jnp.zeros_like(carry)
    width = GROUP * fr_dev

    def multiply(g, _):
        fetch(g).wait()
        x = buf[pl.ds(g * GROUP, GROUP)].astype(jnp.float32) - 7.5
        x = x.astype(jnp.bfloat16).reshape(width, frame)
        both = lax.dot_general(
            w_ref[...], x, (((1,), (1,)), ((), ())), preferred_element_type=jnp.float32
        )
        half = both.shape[0] // 2
        at = pl.ds(pl.multiple_of(g * width, width), width)
        raw[:, at] = both[:half] + both[half:]
        return 0

    parts = min(PARTS, count)
    pairs = in_dev // 2 // parts
    for part in range(parts):
        lax.fori_loop(part * count // parts, (part + 1) * count // parts, multiply, 0)
        for pair in range(part * pairs, (part + 1) * pairs):
            shift_and_add(chans, in_dev, fr_dev, pair, raw, spec, carry)
    extra = o_ref.shape[1] - in_dev - 4
    for c in range(chans):
        block = [spec[c * in_dev : (c + 1) * in_dev]]
        for p in range(2):
            for odd in range(2):
                block.append(carry[odd, p * chans + c : p * chans + c + 1])
        if extra:
            block.append(jnp.zeros((extra, LANES), jnp.float32))
        o_ref[c] = jnp.concatenate(block, axis=0).astype(jnp.bfloat16)


def channelize(samples, chan_index):
    in_dev, fr_dev, frame = samples.shape
    chans = chan_index.shape[0]
    rows = (in_dev + 4 + 15) // 16 * 16
    products = TAPS * 2 * chans
    return pl.pallas_call(
        functools.partial(channelize_kernel, chans),
        in_specs=[
            pl.BlockSpec(memory_space=pltpu.SMEM),
            pl.BlockSpec(memory_space=pl.ANY),
        ],
        out_specs=pl.BlockSpec(memory_space=pltpu.VMEM),
        out_shape=jax.ShapeDtypeStruct((chans, rows, LANES), jnp.bfloat16),
        scratch_shapes=[
            pltpu.VMEM(samples.shape, jnp.int32),
            pltpu.VMEM((2 * products, frame), jnp.bfloat16),
            pltpu.VMEM((products, in_dev * fr_dev), jnp.float32),
            pltpu.VMEM((chans * in_dev, LANES), jnp.float32),
            pltpu.VMEM((2, 2 * chans, LANES), jnp.float32),
            pltpu.SemaphoreType.DMA((in_dev // GROUP,)),
        ],
        compiler_params=pltpu.CompilerParams(vmem_limit_bytes=48 * 2**20),
        name="channelize",
    )(chan_index, samples)


def place_carry(carried, in_dev, fr_dev):
    mine = lax.broadcasted_iota(jnp.int32, (in_dev, LANES), 0)
    lane = lax.broadcasted_iota(jnp.int32, (in_dev, LANES), 1)
    mask = lane // TAPS == mine // 2
    odd = mine % 2 == 1
    src = lax.broadcasted_iota(jnp.int32, (2 * LANES, LANES), 0)
    dst = lax.broadcasted_iota(jnp.int32, (2 * LANES, LANES), 1)
    place = (src // LANES) * fr_dev + src % TAPS
    spread = jnp.where((place == dst) & (src % TAPS < TAPS - 1), 1.0, 0.0).astype(jnp.bfloat16)
    picked = []
    for four in carried:
        both = []
        for p in range(2):
            row = jnp.where(odd, four[2 * p + 1][None], four[2 * p][None])
            both.append(jnp.where(mask, row, 0.0).astype(jnp.bfloat16))
        picked.append(jnp.concatenate(both, axis=1))
    return jnp.dot(
        jnp.concatenate(picked, axis=0), spread, preferred_element_type=jnp.float32
    )


def correlate_kernel(n_freq, n_tm, in_dev, fr_dev, where_ref, *refs):
    sources, (o_ref, left, right, result, sems) = refs[:4], refs[4:]
    n_bl = len(sources)
    me = where_ref[0]
    scale = 1.0 / (n_tm * fr_dev)
    order = [(f, k) for f in range(n_freq // 2) for k in range(n_bl)]
    for out, base in ((left, me // 2 * (n_freq // 2)), (right, me % 2 * (n_freq // 2))):
        for t in range(n_tm):
            blocks = [sources[k][(base + f) * n_tm + t, :in_dev, :] for f, k in order]
            if t:
                carried = [
                    sources[k][(base + f) * n_tm + t - 1, in_dev : in_dev + 4, :].astype(jnp.float32)
                    for f, k in order
                ]
                moved = place_carry(carried, in_dev, fr_dev)
                whole = jnp.concatenate(blocks, axis=0).astype(jnp.float32) + moved
                whole = whole.astype(jnp.bfloat16)
                blocks = [whole[m * in_dev : (m + 1) * in_dev] for m in range(len(order))]
            for (f, k), block in zip(order, blocks):
                at = pl.multiple_of((f * n_bl + (me ^ k)) * in_dev, in_dev)
                out[pl.ds(at, in_dev), t * LANES : (t + 1) * LANES] = block
    half = left.shape[0]
    rows = half // sems.shape[0]
    lane = lax.broadcasted_iota(jnp.int32, (rows, LANES), 1)
    dims = (((1,), (1,)), ((), ()))
    copies = []
    for m in range(sems.shape[0]):
        span = pl.ds(m * rows, rows)
        mine = left[m * rows : (m + 1) * rows, :]
        turned = []
        for t in range(n_tm):
            part = mine[:, t * LANES : (t + 1) * LANES].astype(jnp.float32)
            part = pltpu.roll(part, fr_dev, 1)
            turned.append(jnp.where(lane < fr_dev, part, -part).astype(jnp.bfloat16))
        for p, a in enumerate((mine, jnp.concatenate(turned, axis=1))):
            result[p, m * rows : (m + 1) * rows, :] = scale * lax.dot_general(
                a, right[...], dims, preferred_element_type=jnp.float32
            )
        copies.append(
            pltpu.make_async_copy(
                result.at[:, span], o_ref.at[0, 0, :, span], sems.at[m]
            )
        )
        copies[-1].start()
    for copy in copies:
        copy.wait()


def correlate(sources, me, n_freq, n_tm, in_dev, fr_dev):
    half = n_freq * len(sources) * in_dev // 2
    return pl.pallas_call(
        functools.partial(correlate_kernel, n_freq, n_tm, in_dev, fr_dev),
        in_specs=[pl.BlockSpec(memory_space=pltpu.SMEM)]
        + [pl.BlockSpec(memory_space=pltpu.VMEM)] * len(sources),
        out_specs=pl.BlockSpec(memory_space=pl.ANY),
        out_shape=jax.ShapeDtypeStruct((1, 1, 2, half, half), jnp.float32),
        scratch_shapes=[
            pltpu.VMEM((half, n_tm * LANES), jnp.bfloat16),
            pltpu.VMEM((half, n_tm * LANES), jnp.bfloat16),
            pltpu.VMEM((2, half, half), jnp.float32),
            pltpu.SemaphoreType.DMA((4,)),
        ],
        compiler_params=pltpu.CompilerParams(vmem_limit_bytes=16 * 2**20),
        name="correlate",
    )(me, *sources)


def correlate_plain(gathered, where, n_freq, n_tm, in_dev, fr_dev):
    n_bl = gathered.shape[0]
    half = n_freq * n_bl * in_dev // 2
    blocks = gathered.reshape(n_bl, n_freq, n_tm, -1, LANES)
    blocks = jnp.transpose(blocks, (1, 0, 2, 3, 4)).astype(jnp.float32)
    main = blocks[:, :, :, :in_dev].reshape(n_freq, n_bl, n_tm, in_dev, 2, fr_dev)
    over = blocks[:, :, :-1, in_dev : in_dev + 4, : in_dev // 2 * TAPS]
    over = over.reshape(n_freq, n_bl, n_tm - 1, 2, 2, in_dev // 2, TAPS)
    over = jnp.transpose(over, (0, 1, 2, 5, 4, 3, 6))
    over = over.reshape(n_freq, n_bl, n_tm - 1, in_dev, 2, TAPS)[..., : TAPS - 1]
    over = jnp.pad(over, [(0, 0)] * 2 + [(1, 0)] + [(0, 0)] * 2 + [(0, fr_dev - TAPS + 1)])
    whole = (main + over).astype(jnp.bfloat16)
    whole = jnp.transpose(whole, (4, 0, 1, 3, 2, 5)).reshape(2, 2 * half, n_tm * fr_dev)
    rows = lax.dynamic_slice_in_dim(whole, where[0] * half, half, 1)
    cols = lax.dynamic_slice_in_dim(whole, where[1] * half, half, 1)
    right = jnp.concatenate([cols[0], cols[1]], axis=1)
    left = jnp.stack(
        [jnp.concatenate([rows[0], rows[1]], 1), jnp.concatenate([rows[1], -rows[0]], 1)]
    )
    product = jnp.einsum("phf,qf->phq", left, right, preferred_element_type=jnp.float32)
    return (product / (n_tm * fr_dev))[None, None]


def swapped(block, axis, distance):
    count = lax.axis_size(axis)
    return lax.ppermute(block, axis, [(i, i ^ distance) for i in range(count)])


def on_device(samples, chan_index):
    in_dev, fr_dev, frame = samples.shape
    n_freq = lax.axis_size("freq")
    n_tm = lax.axis_size("tm")
    spectra = channelize(samples, chan_index)
    moved = lax.all_to_all(spectra, ("freq", "tm"), split_axis=0, concat_axis=0, tiled=True)
    tile = lax.axis_index("bl")
    if in_dev % 16 == 0:
        far = swapped(moved, "bl", 2)
        near = swapped(moved, "bl", 1)
        sources = (moved, near, far, swapped(far, "bl", 1))
        return correlate(sources, tile.reshape(1), n_freq, n_tm, in_dev, fr_dev)
    gathered = lax.all_gather(moved, "bl", axis=0, tiled=False)
    where = jnp.stack([tile // 2, tile % 2]).astype(jnp.int32)
    return correlate_plain(gathered, where, n_freq, n_tm, in_dev, fr_dev)


def solution(mesh):
    placed = (P(("freq", "bl"), "tm", None), P())
    return jax.shard_map(
        on_device,
        mesh=mesh,
        in_specs=placed,
        out_specs=P(("freq", "tm"), "bl", None, None, None),
        check_vma=False,
    )
```

```python
import functools
import math

import jax
import jax.numpy as jnp
from jax import lax
from jax.experimental import pallas as pl
from jax.experimental.pallas import tpu as pltpu
from jax.sharding import PartitionSpec as P

TAPS = 4
LANES = 128
GROUP = 4


def bin_column(chan_ref, chans):
    row = lax.broadcasted_iota(jnp.int32, (chans, LANES), 0)
    out = jnp.zeros((chans, LANES), jnp.int32)
    for c in range(chans):
        out = jnp.where(row == c, chan_ref[c], out)
    return out[:, :1]


def build_weights(chan_ref, w_ref, chans):
    frame = w_ref.shape[1]
    half = w_ref.shape[0] // 2
    bins = bin_column(chan_ref, chans)
    steps = lax.broadcasted_iota(jnp.int32, (chans, frame), 1)
    angle = (bins * steps % frame).astype(jnp.float32) * (2.0 * math.pi / frame)
    scale = 1.0 / math.sqrt(frame)
    table = jnp.concatenate([jnp.cos(angle) * scale, -jnp.sin(angle) * scale], axis=0)
    table = table.astype(jnp.bfloat16).astype(jnp.float32) * 0.25
    tap = lax.broadcasted_iota(jnp.int32, (8, frame), 0) % TAPS
    place = lax.broadcasted_iota(jnp.int32, (8, frame), 1) + tap * frame
    place = place.astype(jnp.float32) + 0.5
    turn = math.pi * ((place - 2.0 * frame) / frame)
    window = 0.5 - 0.5 * jnp.cos(place * (2.0 * math.pi / (TAPS * frame)))
    taps = jnp.sin(turn) / turn * window
    rows = 2 * chans
    for k in range(TAPS):
        full = taps[k : k + 1] * table
        high = full.astype(jnp.bfloat16)
        low = (full - high.astype(jnp.float32)).astype(jnp.bfloat16)
        w_ref[k * rows : (k + 1) * rows] = high
        w_ref[half + k * rows : half + (k + 1) * rows] = low


def shift_and_add(chans, in_dev, fr_dev, pair, raw, spec, carry):
    rows = 2 * chans
    lane = lax.broadcasted_iota(jnp.int32, (rows, LANES), 1)
    place = lane % fr_dev
    first = lax.broadcasted_iota(jnp.int32, (chans, LANES), 1) < fr_dev
    span = slice(pair * LANES, (pair + 1) * LANES)
    own = raw[(TAPS - 1) * rows :, span]
    over = jnp.zeros_like(own)
    for k in range(TAPS - 1):
        late = TAPS - 1 - k
        moved = pltpu.roll(raw[k * rows : (k + 1) * rows, span], late, 1)
        own = own + jnp.where(place >= late, moved, 0.0)
        over = over + jnp.where(place < late, moved, 0.0)
    re, im = own[:chans], own[chans:]
    even = jnp.where(first, re, pltpu.roll(im, fr_dev, 1))
    odd = jnp.where(first, pltpu.roll(re, fr_dev, 1), im)
    spec[pl.ds(pair * 2, chans, stride=in_dev), :] = even
    spec[pl.ds(pair * 2 + 1, chans, stride=in_dev), :] = odd
    shift = pair * TAPS
    from_even = jnp.where(lane >= fr_dev, over, 0.0)
    from_odd = jnp.where(lane < fr_dev, over, 0.0)
    carry[0] += pltpu.roll(from_even, (shift + fr_dev) % LANES, 1)
    carry[1] += pltpu.roll(from_odd, shift, 1) if shift else from_odd


def channelize_kernel(chans, relative, mesh_shape, me_ref, chan_hbm, x_ref, *refs):
    outs, refs = refs[: -9], refs[-9:]
    buf, w_ref, raw, spec, carry, edge, chan_ref, sems, chan_sem = refs
    in_dev, fr_dev, frame = x_ref.shape
    n_freq, n_tm, n_bl = mesh_shape
    groups = [(i, GROUP) for i in range(0, in_dev - 2 * GROUP, GROUP)]
    tail = len(groups) * GROUP
    groups += [(i, 2) for i in range(tail, in_dev, 2)]

    def fetch(first, count, sem):
        span = pl.ds(first, count)
        return pltpu.make_async_copy(x_ref.at[span], buf.at[span], sems.at[sem])

    chan_copy = pltpu.make_async_copy(chan_hbm, chan_ref, chan_sem)
    chan_copy.start()
    for g, (first, count) in enumerate(groups):
        fetch(first, count, g).start()
    chan_copy.wait()
    build_weights(chan_ref, w_ref, chans)
    carry[...] = jnp.zeros_like(carry)

    def multiply(first, count, sem):
        fetch(first, count, sem).wait()
        x = buf[pl.ds(first, count)].astype(jnp.float32) - 7.5
        x = x.astype(jnp.bfloat16).reshape(count * fr_dev, frame)
        both = lax.dot_general(
            w_ref[...], x, (((1,), (1,)), ((), ())), preferred_element_type=jnp.float32
        )
        half = both.shape[0] // 2
        at = first * fr_dev
        if not isinstance(first, int):
            at = pl.multiple_of(at, GROUP * fr_dev)
        raw[:, pl.ds(at, count * fr_dev)] = both[:half] + both[half:]

    def step(g, _):
        multiply(g * GROUP, GROUP, g)
        return 0

    def slot(m):
        if not relative:
            return m
        freq, tm = me_ref[0] // (n_tm * n_bl), me_ref[0] // n_bl % n_tm
        return (freq ^ (m // n_tm)) * n_tm + (tm ^ (m % n_tm))

    def emit(first, count):
        for m in range(chans):
            at = slot(m) * in_dev + first
            if relative:
                at = pl.multiple_of(at, 8)
            per = chans // len(outs)
            block = spec[pl.ds(at, count), :].astype(jnp.bfloat16)
            outs[m // per][m % per, first : first + count, :] = block

    done = 0
    while done < tail:
        upto = min(done + 4 * GROUP, tail)
        lax.fori_loop(done // GROUP, upto // GROUP, step, 0)
        for pair in range(done // 2, upto // 2):
            shift_and_add(chans, in_dev, fr_dev, pair, raw, spec, carry)
        done = upto
    early = tail // 16 * 16
    if early:
        emit(0, early)
    for g, (first, count) in enumerate(groups):
        if first >= tail:
            multiply(first, count, g)
            shift_and_add(chans, in_dev, fr_dev, first // 2, raw, spec, carry)
    emit(early, in_dev - early)
    edge[...] = jnp.zeros_like(edge)
    for p in range(2):
        for odd in range(2):
            rows = carry[odd, p * chans : (p + 1) * chans, :]
            edge[pl.ds(2 * p + odd, chans, stride=8), :] = rows
    for m in range(chans):
        per = chans // len(outs)
        at = slot(m) * 8
        if relative:
            at = pl.multiple_of(at, 8)
        count = outs[0].shape[1] - in_dev
        block = edge[pl.ds(at, count), :].astype(jnp.bfloat16)
        outs[m // per][m % per, in_dev:, :] = block


def channelize(samples, chan_index, me, relative, mesh_shape):
    in_dev, fr_dev, frame = samples.shape
    chans = chan_index.shape[0]
    rows = (in_dev + 4 + 7) // 8 * 8
    products = TAPS * 2 * chans
    parts = mesh_shape[0] if relative else 1
    out = jax.ShapeDtypeStruct((chans // parts, rows, LANES), jnp.bfloat16)
    return pl.pallas_call(
        functools.partial(channelize_kernel, chans, relative, mesh_shape),
        in_specs=[
            pl.BlockSpec(memory_space=pltpu.SMEM),
            pl.BlockSpec(memory_space=pltpu.HBM),
            pl.BlockSpec(memory_space=pltpu.HBM),
        ],
        out_specs=[pl.BlockSpec(memory_space=pltpu.VMEM)] * parts,
        out_shape=[out] * parts,
        scratch_shapes=[
            pltpu.VMEM(samples.shape, jnp.int32),
            pltpu.VMEM((2 * products, frame), jnp.bfloat16),
            pltpu.VMEM((products, in_dev * fr_dev), jnp.float32),
            pltpu.VMEM((chans * in_dev, LANES), jnp.float32),
            pltpu.VMEM((2, 2 * chans, LANES), jnp.float32),
            pltpu.VMEM((chans * 8, LANES), jnp.float32),
            pltpu.SMEM((chans,), jnp.int32),
            pltpu.SemaphoreType.DMA((in_dev // 2,)),
            pltpu.SemaphoreType.DMA,
        ],
        compiler_params=pltpu.CompilerParams(vmem_limit_bytes=48 * 2**20),
        name="channelize",
    )(me, chan_index, samples)


def place_carry(carried, in_dev, fr_dev):
    mine = lax.broadcasted_iota(jnp.int32, (in_dev, LANES), 0)
    lane = lax.broadcasted_iota(jnp.int32, (in_dev, LANES), 1)
    mask = lane // TAPS == mine // 2
    odd = mine % 2 == 1
    src = lax.broadcasted_iota(jnp.int32, (2 * LANES, LANES), 0)
    dst = lax.broadcasted_iota(jnp.int32, (2 * LANES, LANES), 1)
    place = (src // LANES) * fr_dev + src % TAPS
    spread = jnp.where((place == dst) & (src % TAPS < TAPS - 1), 1.0, 0.0).astype(jnp.bfloat16)
    picked = []
    for four in carried:
        both = []
        for p in range(2):
            row = jnp.where(odd, four[2 * p + 1][None], four[2 * p][None])
            both.append(jnp.where(mask, row, 0.0).astype(jnp.bfloat16))
        picked.append(jnp.concatenate(both, axis=1))
    return jnp.dot(
        jnp.concatenate(picked, axis=0), spread, preferred_element_type=jnp.float32
    )


def correlate_kernel(mesh_shape, in_dev, fr_dev, me_ref, *refs):
    n_freq, n_tm, n_bl = mesh_shape
    own_half, other_half = refs[:n_bl], refs[n_bl : 2 * n_bl]
    o_ref, left, right, result, sems = refs[2 * n_bl :]
    me = me_ref[0]
    freq, tm, bl = me // (n_tm * n_bl), me // n_bl % n_tm, me % n_bl
    scale = 1.0 / (n_tm * fr_dev)
    order = [(f, k) for f in range(n_freq // 2) for k in range(n_bl)]
    for out, base in ((left, bl // 2 * (n_freq // 2)), (right, bl % 2 * (n_freq // 2))):
        early, late, carried = [], [], []
        for f, k in order:
            at = (base + f) ^ freq
            mine, other = own_half[k], other_half[k]
            body, over = slice(0, in_dev), slice(in_dev, in_dev + 4)
            early.append(jnp.where(tm == 0, mine[at, body, :], other[at, body, :]))
            late.append(jnp.where(tm == 0, other[at, body, :], mine[at, body, :]))
            four = jnp.where(tm == 0, mine[at, over, :], other[at, over, :])
            carried.append(four.astype(jnp.float32))
        late = jnp.concatenate(late, axis=0).astype(jnp.float32)
        late = (late + place_carry(carried, in_dev, fr_dev)).astype(jnp.bfloat16)
        for m, (f, k) in enumerate(order):
            at = pl.multiple_of((f * n_bl + (bl ^ k)) * in_dev, in_dev)
            out[pl.ds(at, in_dev), :LANES] = early[m]
            out[pl.ds(at, in_dev), LANES:] = late[m * in_dev : (m + 1) * in_dev]
    half = left.shape[0]
    rows = half // sems.shape[0]
    lane = lax.broadcasted_iota(jnp.int32, (rows, LANES), 1)
    dims = (((1,), (1,)), ((), ()))
    copies = []
    for m in range(sems.shape[0]):
        span = pl.ds(m * rows, rows)
        mine = left[m * rows : (m + 1) * rows, :]
        turned = []
        for t in range(n_tm):
            part = mine[:, t * LANES : (t + 1) * LANES].astype(jnp.float32)
            part = pltpu.roll(part, fr_dev, 1)
            turned.append(jnp.where(lane < fr_dev, part, -part).astype(jnp.bfloat16))
        for p, a in enumerate((mine, jnp.concatenate(turned, axis=1))):
            result[p, m * rows : (m + 1) * rows, :] = scale * lax.dot_general(
                a, right[...], dims, preferred_element_type=jnp.float32
            )
        copies.append(
            pltpu.make_async_copy(
                result.at[:, span], o_ref.at[0, 0, :, span], sems.at[m]
            )
        )
        copies[-1].start()
    for copy in copies:
        copy.wait()


def correlate(sources, me, mesh_shape, in_dev, fr_dev):
    n_freq, n_tm, n_bl = mesh_shape
    half = n_freq * n_bl * in_dev // 2
    return pl.pallas_call(
        functools.partial(correlate_kernel, mesh_shape, in_dev, fr_dev),
        in_specs=[pl.BlockSpec(memory_space=pltpu.SMEM)]
        + [pl.BlockSpec(memory_space=pltpu.VMEM)] * len(sources),
        out_specs=pl.BlockSpec(memory_space=pl.ANY),
        out_shape=jax.ShapeDtypeStruct((1, 1, 2, half, half), jnp.float32),
        scratch_shapes=[
            pltpu.VMEM((half, n_tm * LANES), jnp.bfloat16),
            pltpu.VMEM((half, n_tm * LANES), jnp.bfloat16),
            pltpu.VMEM((2, half, half), jnp.float32),
            pltpu.SemaphoreType.DMA((4,)),
        ],
        compiler_params=pltpu.CompilerParams(vmem_limit_bytes=16 * 2**20),
        name="correlate",
    )(me, *sources)


def correlate_plain(gathered, where, n_freq, n_tm, in_dev, fr_dev):
    n_bl = gathered.shape[0]
    half = n_freq * n_bl * in_dev // 2
    blocks = gathered.reshape(n_bl, n_freq, n_tm, -1, LANES)
    blocks = jnp.transpose(blocks, (1, 0, 2, 3, 4)).astype(jnp.float32)
    main = blocks[:, :, :, :in_dev].reshape(n_freq, n_bl, n_tm, in_dev, 2, fr_dev)
    over = blocks[:, :, :-1, in_dev : in_dev + 4, : in_dev // 2 * TAPS]
    over = over.reshape(n_freq, n_bl, n_tm - 1, 2, 2, in_dev // 2, TAPS)
    over = jnp.transpose(over, (0, 1, 2, 5, 4, 3, 6))
    over = over.reshape(n_freq, n_bl, n_tm - 1, in_dev, 2, TAPS)[..., : TAPS - 1]
    over = jnp.pad(over, [(0, 0)] * 2 + [(1, 0)] + [(0, 0)] * 2 + [(0, fr_dev - TAPS + 1)])
    whole = (main + over).astype(jnp.bfloat16)
    whole = jnp.transpose(whole, (4, 0, 1, 3, 2, 5)).reshape(2, 2 * half, n_tm * fr_dev)
    rows = lax.dynamic_slice_in_dim(whole, where[0] * half, half, 1)
    cols = lax.dynamic_slice_in_dim(whole, where[1] * half, half, 1)
    right = jnp.concatenate([cols[0], cols[1]], axis=1)
    left = jnp.stack(
        [jnp.concatenate([rows[0], rows[1]], 1), jnp.concatenate([rows[1], -rows[0]], 1)]
    )
    product = jnp.einsum("phf,qf->phq", left, right, preferred_element_type=jnp.float32)
    return (product / (n_tm * fr_dev))[None, None]


def swapped(block, axes, distance):
    count = math.prod(lax.axis_size(axis) for axis in axes)
    return lax.ppermute(block, axes, [(i, i ^ distance) for i in range(count)])


def exchange(parts, n_bl):
    arrived = [parts[0]] + [None] * (len(parts) - 1)
    for k in reversed(range(1, len(parts))):
        arrived[k] = swapped(parts[k], ("freq",), k)
    keep = jnp.stack([block[0] for block in arrived])
    send = jnp.stack([block[1] for block in arrived])
    across = ("tm", "bl")
    corner = swapped(send, across, n_bl + 2)
    beside = swapped(send, across, n_bl)
    far = swapped(keep, across, 2)
    own_half, other_half = [keep, None, far, None], [beside, None, corner, None]
    for half in (own_half, other_half):
        for k in (0, 2):
            half[k + 1] = swapped(half[k], ("bl",), 1)
    return own_half + other_half


def on_device(samples, chan_index):
    in_dev, fr_dev, frame = samples.shape
    axes = ("freq", "tm", "bl")
    mesh_shape = tuple(lax.axis_size(axis) for axis in axes)
    n_freq, n_tm, n_bl = mesh_shape
    me = lax.axis_index(axes).reshape(1)
    relative = in_dev % 16 == 0 and n_freq <= 4 and n_tm == 2 and n_bl == 4
    spectra = channelize(samples, chan_index, me, relative, mesh_shape)
    if relative:
        sources = exchange(spectra, n_bl)
        return correlate(sources, me, mesh_shape, in_dev, fr_dev)
    moved = lax.all_to_all(spectra[0], ("freq", "tm"), split_axis=0, concat_axis=0, tiled=True)
    gathered = lax.all_gather(moved, "bl", axis=0, tiled=False)
    tile = lax.axis_index("bl")
    where = jnp.stack([tile // 2, tile % 2]).astype(jnp.int32)
    return correlate_plain(gathered, where, n_freq, n_tm, in_dev, fr_dev)


def solution(mesh):
    placed = (P(("freq", "bl"), "tm", None), P())
    return jax.shard_map(
        on_device,
        mesh=mesh,
        in_specs=placed,
        out_specs=P(("freq", "tm"), "bl", None, None, None),
        check_vma=False,
    )
```

```python
import functools
import math

import jax
import jax.numpy as jnp
from jax import lax
from jax.experimental import pallas as pl
from jax.experimental.pallas import tpu as pltpu
from jax.sharding import PartitionSpec as P

TAPS = 4
LANES = 128
GROUP = 4
BANK = 16
PIECES = 3
EIGHT = jnp.float8_e4m3fn


def bin_column(chan_ref, chans):
    row = lax.broadcasted_iota(jnp.int32, (chans, LANES), 0)
    out = jnp.zeros((chans, LANES), jnp.int32)
    for c in range(chans):
        out = jnp.where(row == c, chan_ref[c], out)
    return out[:, :1]


def build_weights(chan_ref, w_ref, chans, frame):
    bins = bin_column(chan_ref, chans)
    steps = lax.broadcasted_iota(jnp.int32, (chans, frame), 1)
    angle = (bins * steps % frame).astype(jnp.float32) * (2.0 * math.pi / frame)
    scale = 1.0 / math.sqrt(frame)
    table = jnp.concatenate([jnp.cos(angle) * scale, -jnp.sin(angle) * scale], axis=0)
    units = 2.0 ** math.floor(math.log2(256.0 * 4.0 / scale))
    table = table.astype(jnp.bfloat16).astype(jnp.float32) * (0.25 * units)
    tap = lax.broadcasted_iota(jnp.int32, (8, frame), 0) % TAPS
    place = lax.broadcasted_iota(jnp.int32, (8, frame), 1) + tap * frame
    place = place.astype(jnp.float32) + 0.5
    turn = math.pi * ((place - 2.0 * frame) / frame)
    window = 0.5 - 0.5 * jnp.cos(place * (2.0 * math.pi / (TAPS * frame)))
    taps = jnp.sin(turn) / turn * window
    left = jnp.concatenate([taps[k : k + 1] * table for k in range(TAPS)], axis=0)
    count = left.shape[0]
    for piece in range(PIECES):
        part = left.astype(EIGHT)
        w_ref[piece * count : (piece + 1) * count, :] = part
        left = (left - part.astype(jnp.float32)) * 16.0
    return units


def shift_and_add(chans, in_dev, fr_dev, pair, raw, spec, carry):
    rows = 2 * chans
    lane = lax.broadcasted_iota(jnp.int32, (rows, LANES), 1)
    place = lane % fr_dev
    first = lax.broadcasted_iota(jnp.int32, (chans, LANES), 1) < fr_dev
    span = slice(pair * LANES, (pair + 1) * LANES)
    own = raw[(TAPS - 1) * rows :, span]
    over = jnp.zeros_like(own)
    for k in range(TAPS - 1):
        late = TAPS - 1 - k
        moved = pltpu.roll(raw[k * rows : (k + 1) * rows, span], late, 1)
        own = own + jnp.where(place >= late, moved, 0.0)
        over = over + jnp.where(place < late, moved, 0.0)
    re, im = own[:chans], own[chans:]
    even = jnp.where(first, re, pltpu.roll(im, fr_dev, 1))
    odd = jnp.where(first, pltpu.roll(re, fr_dev, 1), im)
    spec[pl.ds(pair * 2, chans, stride=in_dev), :] = even
    spec[pl.ds(pair * 2 + 1, chans, stride=in_dev), :] = odd
    bank, shift = pair // BANK, pair % BANK * TAPS
    carry[bank] += pltpu.roll(over, shift, 1) if shift else over


def channelize_kernel(chans, relative, mesh_shape, me_ref, chan_hbm, x_ref, *refs):
    outs, refs = refs[: -9], refs[-9:]
    buf, w_ref, raw, spec, carry, edge, chan_ref, sems, chan_sem = refs
    in_dev, fr_dev, frame = x_ref.shape
    n_freq, n_tm, n_bl = mesh_shape
    tail = (in_dev - 1) // GROUP * GROUP
    groups = [(i, GROUP) for i in range(0, tail, GROUP)]
    groups += [(i, 4) for i in range(tail, in_dev, 4)]

    def fetch(first, count, sem):
        span = pl.ds(first, count)
        return pltpu.make_async_copy(x_ref.at[span], buf.at[span], sems.at[sem])

    chan_copy = pltpu.make_async_copy(chan_hbm, chan_ref, chan_sem)
    chan_copy.start()
    for g, (first, count) in enumerate(groups):
        fetch(first, count, g).start()
    chan_copy.wait()
    units = build_weights(chan_ref, w_ref, chans, frame)
    carry[...] = jnp.zeros_like(carry)

    def multiply(first, count, sem):
        fetch(first, count, sem).wait()
        x = buf[pl.ds(first, count)].astype(jnp.float32) - 7.5
        x = x.astype(EIGHT).reshape(count * fr_dev, frame)
        pieces = lax.dot_general(
            w_ref[...], x, (((1,), (1,)), ((), ())), preferred_element_type=jnp.float32
        )
        rows = pieces.shape[0] // PIECES
        total = pieces[:rows] * (1.0 / units)
        for piece in range(1, PIECES):
            total += pieces[piece * rows : (piece + 1) * rows] * (0.0625**piece / units)
        at = first * fr_dev
        if not isinstance(first, int):
            at = pl.multiple_of(at, GROUP * fr_dev)
        raw[:, pl.ds(at, count * fr_dev)] = total

    def step(g, _):
        multiply(g * GROUP, GROUP, g)
        return 0

    def slot(m):
        if not relative:
            return m
        freq, tm = me_ref[0] // (n_tm * n_bl), me_ref[0] // n_bl % n_tm
        return (freq ^ (m // n_tm)) * n_tm + (tm ^ (m % n_tm))

    def emit(first, count):
        for m in range(chans):
            at = slot(m) * in_dev + first
            if relative:
                at = pl.multiple_of(at, 8)
            per = chans // len(outs)
            block = spec[pl.ds(at, count), :].astype(jnp.bfloat16)
            outs[m // per][m % per, first : first + count, :] = block

    done = 0
    while done < tail:
        upto = min(done + 4 * GROUP, tail)
        lax.fori_loop(done // GROUP, upto // GROUP, step, 0)
        for pair in range(done // 2, upto // 2):
            shift_and_add(chans, in_dev, fr_dev, pair, raw, spec, carry)
        done = upto
    early = tail // 16 * 16
    if early:
        emit(0, early)
    for g, (first, count) in enumerate(groups):
        if first >= tail:
            multiply(first, count, g)
            for pair in range(first // 2, (first + count) // 2):
                shift_and_add(chans, in_dev, fr_dev, pair, raw, spec, carry)
    emit(early, in_dev - early)
    edge[...] = jnp.zeros_like(edge)
    for p in range(2):
        for bank in range(2):
            rows = carry[bank, p * chans : (p + 1) * chans, :]
            edge[pl.ds(2 * p + bank, chans, stride=8), :] = rows
    for m in range(chans):
        per = chans // len(outs)
        at = slot(m) * 8
        if relative:
            at = pl.multiple_of(at, 8)
        count = outs[0].shape[1] - in_dev
        block = edge[pl.ds(at, count), :].astype(jnp.bfloat16)
        outs[m // per][m % per, in_dev:, :] = block


def channelize(samples, chan_index, me, relative, mesh_shape):
    in_dev, fr_dev, frame = samples.shape
    chans = chan_index.shape[0]
    rows = (in_dev + 4 + 7) // 8 * 8
    products = TAPS * 2 * chans
    parts = mesh_shape[0] if relative else 1
    out = jax.ShapeDtypeStruct((chans // parts, rows, LANES), jnp.bfloat16)
    chan_index = pltpu.with_memory_space_constraint(chan_index, pltpu.HBM)
    return pl.pallas_call(
        functools.partial(channelize_kernel, chans, relative, mesh_shape),
        in_specs=[
            pl.BlockSpec(memory_space=pltpu.SMEM),
            pl.BlockSpec(memory_space=pltpu.HBM),
            pl.BlockSpec(memory_space=pltpu.HBM),
        ],
        out_specs=[pl.BlockSpec(memory_space=pltpu.VMEM)] * parts,
        out_shape=[out] * parts,
        scratch_shapes=[
            pltpu.VMEM(samples.shape, jnp.int32),
            pltpu.VMEM((PIECES * products, frame), EIGHT),
            pltpu.VMEM((products, in_dev * fr_dev), jnp.float32),
            pltpu.VMEM((chans * in_dev, LANES), jnp.float32),
            pltpu.VMEM((2, 2 * chans, LANES), jnp.float32),
            pltpu.VMEM((chans * 8, LANES), jnp.float32),
            pltpu.SMEM((chans,), jnp.int32),
            pltpu.SemaphoreType.DMA((in_dev // 2,)),
            pltpu.SemaphoreType.DMA,
        ],
        compiler_params=pltpu.CompilerParams(vmem_limit_bytes=48 * 2**20),
        name="channelize",
    )(me, chan_index, samples)


def place_carry(carried, in_dev, fr_dev):
    mine = lax.broadcasted_iota(jnp.int32, (in_dev, LANES), 0)
    lane = lax.broadcasted_iota(jnp.int32, (in_dev, LANES), 1)
    mask = lane // TAPS == mine // 2 % BANK + (1 - mine % 2) * BANK
    second = mine // 2 >= BANK
    src = lax.broadcasted_iota(jnp.int32, (2 * LANES, LANES), 0)
    dst = lax.broadcasted_iota(jnp.int32, (2 * LANES, LANES), 1)
    place = (src // LANES) * fr_dev + src % TAPS
    spread = jnp.where((place == dst) & (src % TAPS < TAPS - 1), 1.0, 0.0).astype(jnp.bfloat16)
    picked = []
    for four in carried:
        both = []
        for p in range(2):
            row = jnp.where(second, four[2 * p + 1][None], four[2 * p][None])
            both.append(jnp.where(mask, row, 0.0).astype(jnp.bfloat16))
        picked.append(jnp.concatenate(both, axis=1))
    return jnp.dot(
        jnp.concatenate(picked, axis=0), spread, preferred_element_type=jnp.float32
    )


def correlate_kernel(mesh_shape, in_dev, fr_dev, me_ref, *refs):
    n_freq, n_tm, n_bl = mesh_shape
    own_half, other_half = refs[:n_bl], refs[n_bl : 2 * n_bl]
    o_ref, left, right, result, sems = refs[2 * n_bl :]
    me = me_ref[0]
    freq, tm, bl = me // (n_tm * n_bl), me // n_bl % n_tm, me % n_bl
    scale = 1.0 / (n_tm * fr_dev)
    order = [(f, k) for f in range(n_freq // 2) for k in range(n_bl)]
    for out, base in ((left, bl // 2 * (n_freq // 2)), (right, bl % 2 * (n_freq // 2))):
        early, late, carried = [], [], []
        for f, k in order:
            at = (base + f) ^ freq
            mine, other = own_half[k], other_half[k]
            body, over = slice(0, in_dev), slice(in_dev, in_dev + 4)
            early.append(jnp.where(tm == 0, mine[at, body, :], other[at, body, :]))
            late.append(jnp.where(tm == 0, other[at, body, :], mine[at, body, :]))
            four = jnp.where(tm == 0, mine[at, over, :], other[at, over, :])
            carried.append(four.astype(jnp.float32))
        late = jnp.concatenate(late, axis=0).astype(jnp.float32)
        late = (late + place_carry(carried, in_dev, fr_dev)).astype(jnp.bfloat16)
        for m, (f, k) in enumerate(order):
            at = pl.multiple_of((f * n_bl + (bl ^ k)) * in_dev, in_dev)
            out[pl.ds(at, in_dev), :LANES] = early[m]
            out[pl.ds(at, in_dev), LANES:] = late[m * in_dev : (m + 1) * in_dev]
    half = left.shape[0]
    rows = half // sems.shape[0]
    lane = lax.broadcasted_iota(jnp.int32, (rows, LANES), 1)
    dims = (((1,), (1,)), ((), ()))
    copies = []
    for m in range(sems.shape[0]):
        span = pl.ds(m * rows, rows)
        mine = left[m * rows : (m + 1) * rows, :]
        turned = []
        for t in range(n_tm):
            part = mine[:, t * LANES : (t + 1) * LANES].astype(jnp.float32)
            part = pltpu.roll(part, fr_dev, 1)
            turned.append(jnp.where(lane < fr_dev, part, -part).astype(jnp.bfloat16))
        for p, a in enumerate((mine, jnp.concatenate(turned, axis=1))):
            result[p, m * rows : (m + 1) * rows, :] = scale * lax.dot_general(
                a, right[...], dims, preferred_element_type=jnp.float32
            )
        copies.append(
            pltpu.make_async_copy(
                result.at[:, span], o_ref.at[0, 0, :, span], sems.at[m]
            )
        )
        copies[-1].start()
    for copy in copies:
        copy.wait()


def correlate(sources, me, mesh_shape, in_dev, fr_dev):
    n_freq, n_tm, n_bl = mesh_shape
    half = n_freq * n_bl * in_dev // 2
    return pl.pallas_call(
        functools.partial(correlate_kernel, mesh_shape, in_dev, fr_dev),
        in_specs=[pl.BlockSpec(memory_space=pltpu.SMEM)]
        + [pl.BlockSpec(memory_space=pltpu.VMEM)] * len(sources),
        out_specs=pl.BlockSpec(memory_space=pl.ANY),
        out_shape=jax.ShapeDtypeStruct((1, 1, 2, half, half), jnp.float32),
        scratch_shapes=[
            pltpu.VMEM((half, n_tm * LANES), jnp.bfloat16),
            pltpu.VMEM((half, n_tm * LANES), jnp.bfloat16),
            pltpu.VMEM((2, half, half), jnp.float32),
            pltpu.SemaphoreType.DMA((4,)),
        ],
        compiler_params=pltpu.CompilerParams(vmem_limit_bytes=16 * 2**20),
        name="correlate",
    )(me, *sources)


def correlate_plain(gathered, where, n_freq, n_tm, in_dev, fr_dev):
    n_bl = gathered.shape[0]
    half = n_freq * n_bl * in_dev // 2
    blocks = gathered.reshape(n_bl, n_freq, n_tm, -1, LANES)
    blocks = jnp.transpose(blocks, (1, 0, 2, 3, 4)).astype(jnp.float32)
    main = blocks[:, :, :, :in_dev].reshape(n_freq, n_bl, n_tm, in_dev, 2, fr_dev)
    over = blocks[:, :, :-1, in_dev : in_dev + 4]
    over = over.reshape(n_freq, n_bl, n_tm - 1, 2, 2, 2, BANK, TAPS)[:, :, :, :, :, ::-1]
    over = jnp.transpose(over, (0, 1, 2, 4, 6, 5, 3, 7))
    over = over.reshape(n_freq, n_bl, n_tm - 1, 4 * BANK, 2, TAPS)[:, :, :, :in_dev, :, : TAPS - 1]
    over = jnp.pad(over, [(0, 0)] * 2 + [(1, 0)] + [(0, 0)] * 2 + [(0, fr_dev - TAPS + 1)])
    whole = (main + over).astype(jnp.bfloat16)
    whole = jnp.transpose(whole, (4, 0, 1, 3, 2, 5)).reshape(2, 2 * half, n_tm * fr_dev)
    rows = lax.dynamic_slice_in_dim(whole, where[0] * half, half, 1)
    cols = lax.dynamic_slice_in_dim(whole, where[1] * half, half, 1)
    right = jnp.concatenate([cols[0], cols[1]], axis=1)
    left = jnp.stack(
        [jnp.concatenate([rows[0], rows[1]], 1), jnp.concatenate([rows[1], -rows[0]], 1)]
    )
    product = jnp.einsum("phf,qf->phq", left, right, preferred_element_type=jnp.float32)
    return (product / (n_tm * fr_dev))[None, None]


def swapped(block, axes, distance):
    count = math.prod(lax.axis_size(axis) for axis in axes)
    return lax.ppermute(block, axes, [(i, i ^ distance) for i in range(count)])


def exchange(parts, n_bl):
    arrived = [parts[0]] + [None] * (len(parts) - 1)
    for k in reversed(range(1, len(parts))):
        arrived[k] = swapped(parts[k], ("freq",), k)
    keep = jnp.stack([block[0] for block in arrived])
    send = jnp.stack([block[1] for block in arrived])
    across = ("tm", "bl")
    corner = swapped(send, across, n_bl + 2)
    beside = swapped(send, across, n_bl)
    far = swapped(keep, across, 2)
    own_half, other_half = [keep, None, far, None], [beside, None, corner, None]
    for half in (own_half, other_half):
        for k in (0, 2):
            half[k + 1] = swapped(half[k], ("bl",), 1)
    return own_half + other_half


def on_device(samples, chan_index):
    in_dev, fr_dev, frame = samples.shape
    axes = ("freq", "tm", "bl")
    mesh_shape = tuple(lax.axis_size(axis) for axis in axes)
    n_freq, n_tm, n_bl = mesh_shape
    me = lax.axis_index(axes).reshape(1)
    relative = in_dev % 16 == 0 and n_freq <= 4 and n_tm == 2 and n_bl == 4
    spectra = channelize(samples, chan_index, me, relative, mesh_shape)
    if relative:
        sources = exchange(spectra, n_bl)
        return correlate(sources, me, mesh_shape, in_dev, fr_dev)
    moved = lax.all_to_all(spectra[0], ("freq", "tm"), split_axis=0, concat_axis=0, tiled=True)
    gathered = lax.all_gather(moved, "bl", axis=0, tiled=False)
    tile = lax.axis_index("bl")
    where = jnp.stack([tile // 2, tile % 2]).astype(jnp.int32)
    return correlate_plain(gathered, where, n_freq, n_tm, in_dev, fr_dev)


def solution(mesh):
    placed = (P(("freq", "bl"), "tm", None), P())
    return jax.shard_map(
        on_device,
        mesh=mesh,
        in_specs=placed,
        out_specs=P(("freq", "tm"), "bl", None, None, None),
        check_vma=False,
    )
```

```python
import functools
import math

import jax
import jax.numpy as jnp
from jax import lax
from jax.experimental import pallas as pl
from jax.experimental.pallas import tpu as pltpu
from jax.sharding import PartitionSpec as P

TAPS = 4
LANES = 128
GROUP = 4
BANK = 16
PIECES = 2
NARROW = jnp.bfloat16
ORDER = (0, 2, 3, 1)


def bin_column(chan_ref, chans):
    row = lax.broadcasted_iota(jnp.int32, (chans, LANES), 0)
    out = jnp.zeros((chans, LANES), jnp.int32)
    for c in range(chans):
        out = jnp.where(row == c, chan_ref[c], out)
    return out[:, :1]


def build_weights(chan_ref, w_ref, chans, frame):
    bins = bin_column(chan_ref, chans)
    steps = lax.broadcasted_iota(jnp.int32, (chans, frame), 1)
    angle = (bins * steps % frame).astype(jnp.float32) * (2.0 * math.pi / frame)
    scale = 1.0 / math.sqrt(frame)
    table = jnp.concatenate([jnp.cos(angle) * scale, -jnp.sin(angle) * scale], axis=0)
    table = table.astype(jnp.bfloat16).astype(jnp.float32) * 0.25
    tap = lax.broadcasted_iota(jnp.int32, (8, frame), 0) % TAPS
    place = lax.broadcasted_iota(jnp.int32, (8, frame), 1) + tap * frame
    place = place.astype(jnp.float32) + 0.5
    turn = math.pi * ((place - 2.0 * frame) / frame)
    window = 0.5 - 0.5 * jnp.cos(place * (2.0 * math.pi / (TAPS * frame)))
    taps = jnp.sin(turn) / turn * window
    left = jnp.concatenate([taps[k : k + 1] * table for k in range(TAPS)], axis=0)
    count = left.shape[0]
    for piece in range(PIECES):
        part = left.astype(NARROW)
        w_ref[piece * count : (piece + 1) * count, :] = part
        left = left - part.astype(jnp.float32)


def shift_and_add(chans, in_dev, fr_dev, pair, raw, spec, carry):
    rows = 2 * chans
    lane = lax.broadcasted_iota(jnp.int32, (rows, LANES), 1)
    place = lane % fr_dev
    first = lax.broadcasted_iota(jnp.int32, (chans, LANES), 1) < fr_dev
    span = slice(pair * LANES, (pair + 1) * LANES)
    own = raw[(TAPS - 1) * rows :, span]
    over = jnp.zeros_like(own)
    for k in range(TAPS - 1):
        late = TAPS - 1 - k
        moved = pltpu.roll(raw[k * rows : (k + 1) * rows, span], late, 1)
        own = own + jnp.where(place >= late, moved, 0.0)
        over = over + jnp.where(place < late, moved, 0.0)
    re, im = own[:chans], own[chans:]
    even = jnp.where(first, re, pltpu.roll(im, fr_dev, 1))
    odd = jnp.where(first, pltpu.roll(re, fr_dev, 1), im)
    spec[pl.ds(pair * 2, chans, stride=in_dev), :] = even
    spec[pl.ds(pair * 2 + 1, chans, stride=in_dev), :] = odd
    bank, shift = pair // BANK, pair % BANK * TAPS
    carry[bank] += pltpu.roll(over, shift, 1) if shift else over


def channelize_kernel(chans, relative, mesh_shape, me_ref, chan_hbm, x_ref, *refs):
    outs, refs = refs[: -9], refs[-9:]
    buf, w_ref, raw, spec, carry, edge, chan_ref, sems, chan_sem = refs
    in_dev, fr_dev, frame = x_ref.shape
    n_freq, n_tm, n_bl = mesh_shape
    tail = (in_dev - 1) // GROUP * GROUP
    groups = [(i, GROUP) for i in range(0, tail, GROUP)]
    groups += [(i, 4) for i in range(tail, in_dev, 4)]

    def fetch(first, count, sem):
        span = pl.ds(first, count)
        return pltpu.make_async_copy(x_ref.at[span], buf.at[span], sems.at[sem])

    chan_copy = pltpu.make_async_copy(chan_hbm, chan_ref, chan_sem)
    chan_copy.start()
    for g, (first, count) in enumerate(groups):
        fetch(first, count, g).start()
    chan_copy.wait()
    build_weights(chan_ref, w_ref, chans, frame)
    carry[...] = jnp.zeros_like(carry)

    def multiply(first, count, sem):
        fetch(first, count, sem).wait()
        x = buf[pl.ds(first, count)].astype(jnp.float32) - 7.5
        x = x.astype(NARROW).reshape(count * fr_dev, frame)
        pieces = lax.dot_general(
            w_ref[...], x, (((1,), (1,)), ((), ())), preferred_element_type=jnp.float32
        )
        rows = pieces.shape[0] // PIECES
        total = pieces[:rows]
        for piece in range(1, PIECES):
            total += pieces[piece * rows : (piece + 1) * rows]
        at = first * fr_dev
        if not isinstance(first, int):
            at = pl.multiple_of(at, GROUP * fr_dev)
        raw[:, pl.ds(at, count * fr_dev)] = total

    def step(g, _):
        multiply(g * GROUP, GROUP, g)
        return 0

    def slot(m):
        if not relative:
            return m
        freq, tm = me_ref[0] // (n_tm * n_bl), me_ref[0] // n_bl % n_tm
        return (freq ^ (m // n_tm)) * n_tm + (tm ^ (m % n_tm))

    def emit(first, count):
        for m in range(chans):
            at = slot(m) * in_dev + first
            if relative:
                at = pl.multiple_of(at, 8)
            per = chans // len(outs)
            block = spec[pl.ds(at, count), :].astype(jnp.bfloat16)
            outs[m // per][m % per, first : first + count, :] = block

    done = 0
    while done < tail:
        upto = min(done + 4 * GROUP, tail)
        lax.fori_loop(done // GROUP, upto // GROUP, step, 0)
        for pair in range(done // 2, upto // 2):
            shift_and_add(chans, in_dev, fr_dev, pair, raw, spec, carry)
        done = upto
    early = tail // 16 * 16
    if early:
        emit(0, early)
    for g, (first, count) in enumerate(groups):
        if first >= tail:
            multiply(first, count, g)
            for pair in range(first // 2, (first + count) // 2):
                shift_and_add(chans, in_dev, fr_dev, pair, raw, spec, carry)
    emit(early, in_dev - early)
    edge[...] = jnp.zeros_like(edge)
    for p in range(2):
        for bank in range(2):
            rows = carry[bank, p * chans : (p + 1) * chans, :]
            edge[pl.ds(2 * p + bank, chans, stride=8), :] = rows
    for m in range(chans):
        per = chans // len(outs)
        at = slot(m) * 8
        if relative:
            at = pl.multiple_of(at, 8)
        count = outs[0].shape[1] - in_dev
        block = edge[pl.ds(at, count), :].astype(jnp.bfloat16)
        outs[m // per][m % per, in_dev:, :] = block


def channelize(samples, chan_index, me, relative, mesh_shape):
    in_dev, fr_dev, frame = samples.shape
    chans = chan_index.shape[0]
    rows = (in_dev + 4 + 7) // 8 * 8
    products = TAPS * 2 * chans
    parts = mesh_shape[0] if relative else 1
    out = jax.ShapeDtypeStruct((chans // parts, rows, LANES), jnp.bfloat16)
    chan_index = pltpu.with_memory_space_constraint(chan_index, pltpu.HBM)
    return pl.pallas_call(
        functools.partial(channelize_kernel, chans, relative, mesh_shape),
        in_specs=[
            pl.BlockSpec(memory_space=pltpu.SMEM),
            pl.BlockSpec(memory_space=pltpu.HBM),
            pl.BlockSpec(memory_space=pltpu.HBM),
        ],
        out_specs=[pl.BlockSpec(memory_space=pltpu.VMEM)] * parts,
        out_shape=[out] * parts,
        scratch_shapes=[
            pltpu.VMEM(samples.shape, jnp.int32),
            pltpu.VMEM((PIECES * products, frame), NARROW),
            pltpu.VMEM((products, in_dev * fr_dev), jnp.float32),
            pltpu.VMEM((chans * in_dev, LANES), jnp.float32),
            pltpu.VMEM((2, 2 * chans, LANES), jnp.float32),
            pltpu.VMEM((chans * 8, LANES), jnp.float32),
            pltpu.SMEM((chans,), jnp.int32),
            pltpu.SemaphoreType.DMA((in_dev // 2,)),
            pltpu.SemaphoreType.DMA,
        ],
        compiler_params=pltpu.CompilerParams(vmem_limit_bytes=48 * 2**20),
        name="channelize",
    )(me, chan_index, samples)


def place_carry(carried, in_dev, fr_dev):
    mine = lax.broadcasted_iota(jnp.int32, (in_dev, LANES), 0)
    lane = lax.broadcasted_iota(jnp.int32, (in_dev, LANES), 1)
    mask = lane // TAPS == mine // 2 % BANK + (1 - mine % 2) * BANK
    second = mine // 2 >= BANK
    src = lax.broadcasted_iota(jnp.int32, (2 * LANES, LANES), 0)
    dst = lax.broadcasted_iota(jnp.int32, (2 * LANES, LANES), 1)
    place = (src // LANES) * fr_dev + src % TAPS
    spread = jnp.where((place == dst) & (src % TAPS < TAPS - 1), 1.0, 0.0).astype(jnp.bfloat16)
    picked = []
    for four in carried:
        both = []
        for p in range(2):
            row = jnp.where(second, four[2 * p + 1][None], four[2 * p][None])
            both.append(jnp.where(mask, row, 0.0).astype(jnp.bfloat16))
        picked.append(jnp.concatenate(both, axis=1))
    return jnp.dot(
        jnp.concatenate(picked, axis=0), spread, preferred_element_type=jnp.float32
    )


def place_of(turn):
    at = jnp.int32(0)
    for place, k in enumerate(ORDER):
        at = jnp.where(turn == k, place, at)
    return at


def correlate_kernel(mesh_shape, in_dev, fr_dev, me_ref, *refs):
    n_freq, n_tm, n_bl = mesh_shape
    own_half, other_half = refs[:n_bl], refs[n_bl : 2 * n_bl]
    o_ref, left, right, result, sems = refs[2 * n_bl :]
    me = me_ref[0]
    freq, tm, bl = me // (n_tm * n_bl), me // n_bl % n_tm, me % n_bl
    scale = 1.0 / (n_tm * fr_dev)
    order = [(f, k) for f in range(n_freq // 2) for k in range(n_bl)]
    for out, base in ((left, bl // 2 * (n_freq // 2)), (right, bl % 2 * (n_freq // 2))):
        early, late, carried = [], [], []
        for f, k in order:
            at = place_of((base + f) ^ freq)
            mine, other = own_half[k], other_half[k]
            body, over = slice(0, in_dev), slice(in_dev, in_dev + 4)
            early.append(jnp.where(tm == 0, mine[at, body, :], other[at, body, :]))
            late.append(jnp.where(tm == 0, other[at, body, :], mine[at, body, :]))
            four = jnp.where(tm == 0, mine[at, over, :], other[at, over, :])
            carried.append(four.astype(jnp.float32))
        late = jnp.concatenate(late, axis=0).astype(jnp.float32)
        late = (late + place_carry(carried, in_dev, fr_dev)).astype(jnp.bfloat16)
        for m, (f, k) in enumerate(order):
            at = pl.multiple_of((f * n_bl + (bl ^ k)) * in_dev, in_dev)
            out[pl.ds(at, in_dev), :LANES] = early[m]
            out[pl.ds(at, in_dev), LANES:] = late[m * in_dev : (m + 1) * in_dev]
    half = left.shape[0]
    rows = half // sems.shape[0]
    lane = lax.broadcasted_iota(jnp.int32, (rows, LANES), 1)
    dims = (((1,), (1,)), ((), ()))
    copies = []
    for m in range(sems.shape[0]):
        span = pl.ds(m * rows, rows)
        mine = left[m * rows : (m + 1) * rows, :]
        turned = []
        for t in range(n_tm):
            part = mine[:, t * LANES : (t + 1) * LANES].astype(jnp.float32)
            part = pltpu.roll(part, fr_dev, 1)
            turned.append(jnp.where(lane < fr_dev, part, -part).astype(jnp.bfloat16))
        for p, a in enumerate((mine, jnp.concatenate(turned, axis=1))):
            result[p, m * rows : (m + 1) * rows, :] = scale * lax.dot_general(
                a, right[...], dims, preferred_element_type=jnp.float32
            )
        copies.append(
            pltpu.make_async_copy(
                result.at[:, span], o_ref.at[0, 0, :, span], sems.at[m]
            )
        )
        copies[-1].start()
    for copy in copies:
        copy.wait()


def correlate(sources, me, mesh_shape, in_dev, fr_dev):
    n_freq, n_tm, n_bl = mesh_shape
    half = n_freq * n_bl * in_dev // 2
    return pl.pallas_call(
        functools.partial(correlate_kernel, mesh_shape, in_dev, fr_dev),
        in_specs=[pl.BlockSpec(memory_space=pltpu.SMEM)]
        + [pl.BlockSpec(memory_space=pltpu.VMEM)] * len(sources),
        out_specs=pl.BlockSpec(memory_space=pl.ANY),
        out_shape=jax.ShapeDtypeStruct((1, 1, 2, half, half), jnp.float32),
        scratch_shapes=[
            pltpu.VMEM((half, n_tm * LANES), jnp.bfloat16),
            pltpu.VMEM((half, n_tm * LANES), jnp.bfloat16),
            pltpu.VMEM((2, half, half), jnp.float32),
            pltpu.SemaphoreType.DMA((4,)),
        ],
        compiler_params=pltpu.CompilerParams(vmem_limit_bytes=16 * 2**20),
        name="correlate",
    )(me, *sources)


def correlate_plain(gathered, where, n_freq, n_tm, in_dev, fr_dev):
    n_bl = gathered.shape[0]
    half = n_freq * n_bl * in_dev // 2
    blocks = gathered.reshape(n_bl, n_freq, n_tm, -1, LANES)
    blocks = jnp.transpose(blocks, (1, 0, 2, 3, 4)).astype(jnp.float32)
    main = blocks[:, :, :, :in_dev].reshape(n_freq, n_bl, n_tm, in_dev, 2, fr_dev)
    over = blocks[:, :, :-1, in_dev : in_dev + 4]
    over = over.reshape(n_freq, n_bl, n_tm - 1, 2, 2, 2, BANK, TAPS)[:, :, :, :, :, ::-1]
    over = jnp.transpose(over, (0, 1, 2, 4, 6, 5, 3, 7))
    over = over.reshape(n_freq, n_bl, n_tm - 1, 4 * BANK, 2, TAPS)[:, :, :, :in_dev, :, : TAPS - 1]
    over = jnp.pad(over, [(0, 0)] * 2 + [(1, 0)] + [(0, 0)] * 2 + [(0, fr_dev - TAPS + 1)])
    whole = (main + over).astype(jnp.bfloat16)
    whole = jnp.transpose(whole, (4, 0, 1, 3, 2, 5)).reshape(2, 2 * half, n_tm * fr_dev)
    rows = lax.dynamic_slice_in_dim(whole, where[0] * half, half, 1)
    cols = lax.dynamic_slice_in_dim(whole, where[1] * half, half, 1)
    right = jnp.concatenate([cols[0], cols[1]], axis=1)
    left = jnp.stack(
        [jnp.concatenate([rows[0], rows[1]], 1), jnp.concatenate([rows[1], -rows[0]], 1)]
    )
    product = jnp.einsum("phf,qf->phq", left, right, preferred_element_type=jnp.float32)
    return (product / (n_tm * fr_dev))[None, None]


def swapped(block, axes, distance):
    count = math.prod(lax.axis_size(axis) for axis in axes)
    return lax.ppermute(block, axes, [(i, i ^ distance) for i in range(count)])


def exchange(parts, n_bl):
    arrived = [parts[0]] + [None] * (len(parts) - 1)
    for k in reversed(range(1, len(parts))):
        arrived[k] = swapped(parts[k], ("freq",), k)
    keep = jnp.stack([arrived[k][0] for k in ORDER])
    send = jnp.stack([arrived[k][1] for k in ORDER])
    across = ("tm", "bl")
    corner = swapped(send, across, n_bl + 2)
    beside = swapped(send, across, n_bl)
    far = swapped(keep, across, 2)
    own_half, other_half = [keep, None, far, None], [beside, None, corner, None]
    for half in (own_half, other_half):
        for k in (0, 2):
            half[k + 1] = swapped(half[k], ("bl",), 1)
    return own_half + other_half


def on_device(samples, chan_index):
    in_dev, fr_dev, frame = samples.shape
    axes = ("freq", "tm", "bl")
    mesh_shape = tuple(lax.axis_size(axis) for axis in axes)
    n_freq, n_tm, n_bl = mesh_shape
    me = lax.axis_index(axes).reshape(1)
    relative = in_dev % 16 == 0 and n_freq <= 4 and n_tm == 2 and n_bl == 4
    spectra = channelize(samples, chan_index, me, relative, mesh_shape)
    if relative:
        sources = exchange(spectra, n_bl)
        return correlate(sources, me, mesh_shape, in_dev, fr_dev)
    moved = lax.all_to_all(spectra[0], ("freq", "tm"), split_axis=0, concat_axis=0, tiled=True)
    gathered = lax.all_gather(moved, "bl", axis=0, tiled=False)
    tile = lax.axis_index("bl")
    where = jnp.stack([tile // 2, tile % 2]).astype(jnp.int32)
    return correlate_plain(gathered, where, n_freq, n_tm, in_dev, fr_dev)


def solution(mesh):
    placed = (P(("freq", "bl"), "tm", None), P())
    return jax.shard_map(
        on_device,
        mesh=mesh,
        in_specs=placed,
        out_specs=P(("freq", "tm"), "bl", None, None, None),
        check_vma=False,
    )
```

```python
import functools
import math

import jax
import jax.numpy as jnp
from jax import lax
from jax.experimental import pallas as pl
from jax.experimental.pallas import tpu as pltpu
from jax.sharding import PartitionSpec as P

TAPS = 4
LANES = 128
GROUP = 4
BANK = 16
PIECES = 2
NARROW = jnp.bfloat16
ORDER = (0, 1, 2, 3)


def bin_column(chan_ref, chans):
    row = lax.broadcasted_iota(jnp.int32, (chans, LANES), 0)
    out = jnp.zeros((chans, LANES), jnp.int32)
    for c in range(chans):
        out = jnp.where(row == c, chan_ref[c], out)
    return out[:, :1]


def build_weights(chan_ref, w_ref, chans, frame):
    bins = bin_column(chan_ref, chans)
    steps = lax.broadcasted_iota(jnp.int32, (chans, frame), 1)
    angle = (bins * steps % frame).astype(jnp.float32) * (2.0 * math.pi / frame)
    scale = 1.0 / math.sqrt(frame)
    table = jnp.concatenate([jnp.cos(angle) * scale, -jnp.sin(angle) * scale], axis=0)
    table = table.astype(jnp.bfloat16).astype(jnp.float32) * 0.25
    tap = lax.broadcasted_iota(jnp.int32, (8, frame), 0) % TAPS
    place = lax.broadcasted_iota(jnp.int32, (8, frame), 1) + tap * frame
    place = place.astype(jnp.float32) + 0.5
    turn = math.pi * ((place - 2.0 * frame) / frame)
    window = 0.5 - 0.5 * jnp.cos(place * (2.0 * math.pi / (TAPS * frame)))
    taps = jnp.sin(turn) / turn * window
    left = jnp.concatenate([taps[k : k + 1] * table for k in range(TAPS)], axis=0)
    count = left.shape[0]
    for piece in range(PIECES):
        part = left.astype(NARROW)
        w_ref[piece * count : (piece + 1) * count, :] = part
        left = left - part.astype(jnp.float32)


def shift_and_add(chans, in_dev, fr_dev, pair, part, spec, carry, keep):
    rows = 2 * chans
    lane = lax.broadcasted_iota(jnp.int32, (rows, LANES), 1)
    place = lane % fr_dev
    first = lax.broadcasted_iota(jnp.int32, (chans, LANES), 1) < fr_dev
    own = part[(TAPS - 1) * rows :]
    over = jnp.zeros_like(own)
    for k in range(TAPS - 1):
        late = TAPS - 1 - k
        moved = pltpu.roll(part[k * rows : (k + 1) * rows], late, 1)
        own = own + jnp.where(place >= late, moved, 0.0)
        over = over + jnp.where(place < late, moved, 0.0)
    re, im = own[:chans], own[chans:]
    even = jnp.where(first, re, pltpu.roll(im, fr_dev, 1))
    odd = jnp.where(first, pltpu.roll(re, fr_dev, 1), im)
    spec[pl.ds(pair * 2, chans, stride=in_dev), :] = even
    spec[pl.ds(pair * 2 + 1, chans, stride=in_dev), :] = odd
    over = jnp.where(keep, pltpu.roll(over, pair % BANK * TAPS, 1), 0.0)
    carry[pair // BANK] += over


def channelize_kernel(chans, relative, mesh_shape, chan_hbm, x_ref, *refs):
    outs, refs = refs[: -9], refs[-9:]
    buf, w_ref, raw, spec, carry, edge, chan_ref, sems, chan_sem = refs
    in_dev, fr_dev, frame = x_ref.shape
    n_freq, n_tm, n_bl = mesh_shape
    def fetch(first, count, sem):
        span = pl.ds(first, count)
        return pltpu.make_async_copy(x_ref.at[span], buf.at[span], sems.at[sem])

    chan_copy = pltpu.make_async_copy(chan_hbm, chan_ref, chan_sem)
    chan_copy.start()
    for g in range(in_dev // GROUP):
        fetch(g * GROUP, GROUP, g).start()
    chan_copy.wait()
    build_weights(chan_ref, w_ref, chans, frame)
    carry[...] = jnp.zeros_like(carry)

    def multiply(g):
        fetch(g * GROUP, GROUP, g).wait()
        x = buf[pl.ds(g * GROUP, GROUP)].astype(jnp.float32) - 7.5
        x = x.astype(NARROW).reshape(GROUP * fr_dev, frame)
        pieces = lax.dot_general(
            w_ref[...], x, (((1,), (1,)), ((), ())), preferred_element_type=jnp.float32
        )
        rows = pieces.shape[0] // PIECES
        total = pieces[:rows]
        for piece in range(1, PIECES):
            total += pieces[piece * rows : (piece + 1) * rows]
        return total

    def finish(g, keep):
        for i in range(GROUP // 2):
            part = raw[g % 2, :, i * LANES : (i + 1) * LANES]
            pair = g * (GROUP // 2) + i
            shift_and_add(chans, in_dev, fr_dev, pair, part, spec, carry, keep)

    def step(g, _):
        total = multiply(g)
        finish(jnp.maximum(g - 1, 0), g > 0)
        raw[g % 2] = total
        return 0

    def slot(m):
        if not relative:
            return m
        freq, tm = lax.axis_index("freq"), lax.axis_index("tm")
        return label((label(freq) + m // n_tm) % n_freq) * n_tm + (tm ^ (m % n_tm))

    def emit(first, count):
        for m in range(chans):
            at = slot(m) * in_dev + first
            if relative:
                at = pl.multiple_of(at, 8)
            per = chans // len(outs)
            block = spec[pl.ds(at, count), :].astype(jnp.bfloat16)
            outs[m // per][m % per, first : first + count, :] = block

    count = in_dev // GROUP
    lax.fori_loop(0, count, step, 0)
    finish(count - 1, True)
    emit(0, in_dev)
    edge[...] = jnp.zeros_like(edge)
    for p in range(2):
        for bank in range(2):
            rows = carry[bank, p * chans : (p + 1) * chans, :]
            edge[pl.ds(2 * p + bank, chans, stride=8), :] = rows
    for m in range(chans):
        per = chans // len(outs)
        at = slot(m) * 8
        if relative:
            at = pl.multiple_of(at, 8)
        count = outs[0].shape[1] - in_dev
        block = edge[pl.ds(at, count), :].astype(jnp.bfloat16)
        outs[m // per][m % per, in_dev:, :] = block


def channelize(samples, chan_index, me, relative, mesh_shape):
    in_dev, fr_dev, frame = samples.shape
    chans = chan_index.shape[0]
    rows = (in_dev + 4 + 7) // 8 * 8
    products = TAPS * 2 * chans
    parts = mesh_shape[0] if relative else 1
    out = jax.ShapeDtypeStruct((chans // parts, rows, LANES), jnp.bfloat16)
    chan_index = pltpu.with_memory_space_constraint(chan_index, pltpu.HBM)
    return pl.pallas_call(
        functools.partial(channelize_kernel, chans, relative, mesh_shape),
        in_specs=[
            pl.BlockSpec(memory_space=pltpu.HBM),
            pl.BlockSpec(memory_space=pltpu.HBM),
        ],
        out_specs=[pl.BlockSpec(memory_space=pltpu.VMEM)] * parts,
        out_shape=[out] * parts,
        scratch_shapes=[
            pltpu.VMEM(samples.shape, jnp.int32),
            pltpu.VMEM((PIECES * products, frame), NARROW),
            pltpu.VMEM((2, products, GROUP * fr_dev), jnp.float32),
            pltpu.VMEM((chans * in_dev, LANES), jnp.float32),
            pltpu.VMEM((2, 2 * chans, LANES), jnp.float32),
            pltpu.VMEM((chans * 8, LANES), jnp.float32),
            pltpu.SMEM((chans,), jnp.int32),
            pltpu.SemaphoreType.DMA((in_dev // 2,)),
            pltpu.SemaphoreType.DMA,
        ],
        compiler_params=pltpu.CompilerParams(vmem_limit_bytes=48 * 2**20),
        name="channelize",
    )(chan_index, samples)


def place_carry(carried, in_dev, fr_dev):
    mine = lax.broadcasted_iota(jnp.int32, (in_dev, LANES), 0)
    lane = lax.broadcasted_iota(jnp.int32, (in_dev, LANES), 1)
    mask = lane // TAPS == mine // 2 % BANK + (1 - mine % 2) * BANK
    second = mine // 2 >= BANK
    src = lax.broadcasted_iota(jnp.int32, (2 * LANES, LANES), 0)
    dst = lax.broadcasted_iota(jnp.int32, (2 * LANES, LANES), 1)
    place = (src // LANES) * fr_dev + src % TAPS
    spread = jnp.where((place == dst) & (src % TAPS < TAPS - 1), 1.0, 0.0).astype(jnp.bfloat16)
    picked = []
    for four in carried:
        both = []
        for p in range(2):
            row = jnp.where(second, four[2 * p + 1][None], four[2 * p][None])
            both.append(jnp.where(mask, row, 0.0).astype(jnp.bfloat16))
        picked.append(jnp.concatenate(both, axis=1))
    return jnp.dot(
        jnp.concatenate(picked, axis=0), spread, preferred_element_type=jnp.float32
    )


def label(z):
    return z ^ (z // 2)


def place_of(turn):
    at = jnp.int32(0)
    for place, k in enumerate(ORDER):
        at = jnp.where(turn == k, place, at)
    return at


def correlate_kernel(mesh_shape, in_dev, fr_dev, *refs):
    n_freq, n_tm, n_bl = mesh_shape
    own_half, other_half = refs[:n_bl], refs[n_bl : 2 * n_bl]
    o_ref, left, right, result, sems = refs[2 * n_bl :]
    freq, tm, bl = (lax.axis_index(axis) for axis in ("freq", "tm", "bl"))
    scale = 1.0 / (n_tm * fr_dev)
    order = [(f, k) for f in range(n_freq // 2) for k in range(n_bl)]
    for out, base in ((left, bl // 2 * (n_freq // 2)), (right, bl % 2 * (n_freq // 2))):
        early, late, carried = [], [], []
        for f, k in order:
            at = place_of((label(freq) - label(base + f) + n_freq) % n_freq)
            mine, other = own_half[k], other_half[k]
            body, over = slice(0, in_dev), slice(in_dev, in_dev + 4)
            early.append(jnp.where(tm == 0, mine[at, body, :], other[at, body, :]))
            late.append(jnp.where(tm == 0, other[at, body, :], mine[at, body, :]))
            four = jnp.where(tm == 0, mine[at, over, :], other[at, over, :])
            carried.append(four.astype(jnp.float32))
        late = jnp.concatenate(late, axis=0).astype(jnp.float32)
        late = (late + place_carry(carried, in_dev, fr_dev)).astype(jnp.bfloat16)
        for m, (f, k) in enumerate(order):
            at = pl.multiple_of((f * n_bl + (bl ^ k)) * in_dev, in_dev)
            out[pl.ds(at, in_dev), :LANES] = early[m]
            out[pl.ds(at, in_dev), LANES:] = late[m * in_dev : (m + 1) * in_dev]
    half = left.shape[0]
    count = sems.shape[0] // 2
    rows = half // count
    lane = lax.broadcasted_iota(jnp.int32, (rows, LANES), 1)
    dims = (((1,), (1,)), ((), ()))
    copies = []
    for m in range(count):
        span = pl.ds(m * rows, rows)
        mine = left[m * rows : (m + 1) * rows, :]
        turned = []
        for t in range(n_tm):
            part = mine[:, t * LANES : (t + 1) * LANES].astype(jnp.float32)
            part = pltpu.roll(part, fr_dev, 1)
            turned.append(jnp.where(lane < fr_dev, part, -part).astype(jnp.bfloat16))
        for p, a in enumerate((mine, jnp.concatenate(turned, axis=1))):
            result[p, m * rows : (m + 1) * rows, :] = scale * lax.dot_general(
                a, right[...], dims, preferred_element_type=jnp.float32
            )
            copies.append(
                pltpu.make_async_copy(result.at[p, span], o_ref.at[0, 0, p, span], sems.at[2 * m + p])
            )
            copies[-1].start()
    for copy in copies:
        copy.wait()


def correlate(sources, me, mesh_shape, in_dev, fr_dev):
    n_freq, n_tm, n_bl = mesh_shape
    half = n_freq * n_bl * in_dev // 2
    return pl.pallas_call(
        functools.partial(correlate_kernel, mesh_shape, in_dev, fr_dev),
        in_specs=[pl.BlockSpec(memory_space=pltpu.VMEM)] * len(sources),
        out_specs=pl.BlockSpec(memory_space=pl.ANY),
        out_shape=jax.ShapeDtypeStruct((1, 1, 2, half, half), jnp.float32),
        scratch_shapes=[
            pltpu.VMEM((half, n_tm * LANES), jnp.bfloat16),
            pltpu.VMEM((half, n_tm * LANES), jnp.bfloat16),
            pltpu.VMEM((2, half, half), jnp.float32),
            pltpu.SemaphoreType.DMA((4,)),
        ],
        compiler_params=pltpu.CompilerParams(vmem_limit_bytes=16 * 2**20),
        name="correlate",
    )(*sources)


def correlate_plain(gathered, where, n_freq, n_tm, in_dev, fr_dev):
    n_bl = gathered.shape[0]
    half = n_freq * n_bl * in_dev // 2
    blocks = gathered.reshape(n_bl, n_freq, n_tm, -1, LANES)
    blocks = jnp.transpose(blocks, (1, 0, 2, 3, 4)).astype(jnp.float32)
    main = blocks[:, :, :, :in_dev].reshape(n_freq, n_bl, n_tm, in_dev, 2, fr_dev)
    over = blocks[:, :, :-1, in_dev : in_dev + 4]
    over = over.reshape(n_freq, n_bl, n_tm - 1, 2, 2, 2, BANK, TAPS)[:, :, :, :, :, ::-1]
    over = jnp.transpose(over, (0, 1, 2, 4, 6, 5, 3, 7))
    over = over.reshape(n_freq, n_bl, n_tm - 1, 4 * BANK, 2, TAPS)[:, :, :, :in_dev, :, : TAPS - 1]
    over = jnp.pad(over, [(0, 0)] * 2 + [(1, 0)] + [(0, 0)] * 2 + [(0, fr_dev - TAPS + 1)])
    whole = (main + over).astype(jnp.bfloat16)
    whole = jnp.transpose(whole, (4, 0, 1, 3, 2, 5)).reshape(2, 2 * half, n_tm * fr_dev)
    rows = lax.dynamic_slice_in_dim(whole, where[0] * half, half, 1)
    cols = lax.dynamic_slice_in_dim(whole, where[1] * half, half, 1)
    right = jnp.concatenate([cols[0], cols[1]], axis=1)
    left = jnp.stack(
        [jnp.concatenate([rows[0], rows[1]], 1), jnp.concatenate([rows[1], -rows[0]], 1)]
    )
    product = jnp.einsum("phf,qf->phq", left, right, preferred_element_type=jnp.float32)
    return (product / (n_tm * fr_dev))[None, None]


def swapped(block, axes, distance):
    count = math.prod(lax.axis_size(axis) for axis in axes)
    return lax.ppermute(block, axes, [(i, i ^ distance) for i in range(count)])


def exchange(parts, n_bl):
    arrived = [parts[0]] + [None] * (len(parts) - 1)
    for k in reversed(range(1, len(parts))):
        arrived[k] = lax.ppermute(parts[k], "freq", [(label(i), label((i + k) % len(parts))) for i in range(len(parts))])
    keep = jnp.stack([arrived[k][0] for k in ORDER])
    send = jnp.stack([arrived[k][1] for k in ORDER])
    across = ("tm", "bl")
    corner = swapped(send, across, n_bl + 2)
    beside = swapped(send, across, n_bl)
    far = swapped(keep, across, 2)
    own_half, other_half = [keep, None, far, None], [beside, None, corner, None]
    for half in (own_half, other_half):
        for k in (0, 2):
            half[k + 1] = swapped(half[k], ("bl",), 1)
    return own_half + other_half


def on_device(samples, chan_index):
    in_dev, fr_dev, frame = samples.shape
    axes = ("freq", "tm", "bl")
    mesh_shape = tuple(lax.axis_size(axis) for axis in axes)
    n_freq, n_tm, n_bl = mesh_shape
    me = lax.axis_index(axes).reshape(1)
    relative = in_dev % 16 == 0 and n_freq <= 4 and n_tm == 2 and n_bl == 4
    spectra = channelize(samples, chan_index, me, relative, mesh_shape)
    if relative:
        sources = exchange(spectra, n_bl)
        return correlate(sources, me, mesh_shape, in_dev, fr_dev)
    moved = lax.all_to_all(spectra[0], ("freq", "tm"), split_axis=0, concat_axis=0, tiled=True)
    gathered = lax.all_gather(moved, "bl", axis=0, tiled=False)
    tile = lax.axis_index("bl")
    where = jnp.stack([tile // 2, tile % 2]).astype(jnp.int32)
    return correlate_plain(gathered, where, n_freq, n_tm, in_dev, fr_dev)


def solution(mesh):
    placed = (P(("freq", "bl"), "tm", None), P())
    return jax.shard_map(
        on_device,
        mesh=mesh,
        in_specs=placed,
        out_specs=P(("freq", "tm"), "bl", None, None, None),
        check_vma=False,
    )
```

```python
import functools
import math

import jax
import jax.numpy as jnp
from jax import lax
from jax.experimental import pallas as pl
from jax.experimental.pallas import tpu as pltpu
from jax.sharding import PartitionSpec as P

TAPS = 4
LANES = 128
GROUP = 4
BANK = 16
PIECES = 2
NARROW = jnp.bfloat16
ORDER = (0, 1, 2, 3)


def bin_column(chan_ref, chans):
    row = lax.broadcasted_iota(jnp.int32, (chans, LANES), 0)
    out = jnp.zeros((chans, LANES), jnp.int32)
    for c in range(chans):
        out = jnp.where(row == c, chan_ref[c], out)
    return out[:, :1]


def build_weights(chan_ref, w_ref, chans, frame):
    bins = bin_column(chan_ref, chans)
    steps = lax.broadcasted_iota(jnp.int32, (chans, frame), 1)
    angle = (bins * steps % frame).astype(jnp.float32) * (2.0 * math.pi / frame)
    scale = 1.0 / math.sqrt(frame)
    table = jnp.concatenate([jnp.cos(angle) * scale, -jnp.sin(angle) * scale], axis=0)
    table = table.astype(jnp.bfloat16).astype(jnp.float32) * 0.25
    tap = lax.broadcasted_iota(jnp.int32, (8, frame), 0) % TAPS
    place = lax.broadcasted_iota(jnp.int32, (8, frame), 1) + tap * frame
    place = place.astype(jnp.float32) + 0.5
    turn = math.pi * ((place - 2.0 * frame) / frame)
    window = 0.5 - 0.5 * jnp.cos(place * (2.0 * math.pi / (TAPS * frame)))
    taps = jnp.sin(turn) / turn * window
    left = jnp.concatenate([taps[k : k + 1] * table for k in range(TAPS)], axis=0)
    count = left.shape[0]
    for piece in range(PIECES):
        part = left.astype(NARROW)
        w_ref[piece * count : (piece + 1) * count, :] = part
        left = left - part.astype(jnp.float32)


def shift_and_add(chans, in_dev, fr_dev, pair, part, spec, carry, keep):
    rows = 2 * chans
    lane = lax.broadcasted_iota(jnp.int32, (rows, LANES), 1)
    place = lane % fr_dev
    first = lax.broadcasted_iota(jnp.int32, (chans, LANES), 1) < fr_dev
    own = part[(TAPS - 1) * rows :]
    over = jnp.zeros_like(own)
    for k in range(TAPS - 1):
        late = TAPS - 1 - k
        moved = pltpu.roll(part[k * rows : (k + 1) * rows], late, 1)
        own = own + jnp.where(place >= late, moved, 0.0)
        over = over + jnp.where(place < late, moved, 0.0)
    re, im = own[:chans], own[chans:]
    even = jnp.where(first, re, pltpu.roll(im, fr_dev, 1))
    odd = jnp.where(first, pltpu.roll(re, fr_dev, 1), im)
    spec[pl.ds(pair * 2, chans, stride=in_dev), :] = even
    spec[pl.ds(pair * 2 + 1, chans, stride=in_dev), :] = odd
    over = jnp.where(keep, pltpu.roll(over, pair % BANK * TAPS, 1), 0.0)
    carry[pair // BANK] += over


def channelize_kernel(chans, relative, mesh_shape, chan_hbm, x_ref, *refs):
    outs, refs = refs[: -9], refs[-9:]
    buf, w_ref, raw, spec, carry, edge, chan_ref, sems, chan_sem = refs
    in_dev, fr_dev, frame = x_ref.shape
    n_freq, n_tm, n_bl = mesh_shape
    def fetch(first, count, sem):
        span = pl.ds(first, count)
        return pltpu.make_async_copy(x_ref.at[span], buf.at[span], sems.at[sem])

    chan_copy = pltpu.make_async_copy(chan_hbm, chan_ref, chan_sem)
    chan_copy.start()
    for g in range(in_dev // GROUP):
        fetch(g * GROUP, GROUP, g).start()
    chan_copy.wait()
    build_weights(chan_ref, w_ref, chans, frame)
    carry[...] = jnp.zeros_like(carry)

    def multiply(g):
        fetch(g * GROUP, GROUP, g).wait()
        x = buf[pl.ds(g * GROUP, GROUP)].astype(jnp.float32) - 7.5
        x = x.astype(NARROW).reshape(GROUP * fr_dev, frame)
        pieces = lax.dot_general(
            w_ref[...], x, (((1,), (1,)), ((), ())), preferred_element_type=jnp.float32
        )
        rows = pieces.shape[0] // PIECES
        total = pieces[:rows]
        for piece in range(1, PIECES):
            total += pieces[piece * rows : (piece + 1) * rows]
        return total

    def finish(g, keep):
        for i in range(GROUP // 2):
            part = raw[g % 2, :, i * LANES : (i + 1) * LANES]
            pair = g * (GROUP // 2) + i
            shift_and_add(chans, in_dev, fr_dev, pair, part, spec, carry, keep)

    def step(g, _):
        total = multiply(g)
        finish(jnp.maximum(g - 1, 0), g > 0)
        raw[g % 2] = total
        return 0

    def slot(m):
        if not relative:
            return m
        freq, tm = lax.axis_index("freq"), lax.axis_index("tm")
        return label((label(freq) + m // n_tm) % n_freq) * n_tm + (tm ^ (m % n_tm))

    def emit(first, count):
        for m in range(chans):
            at = slot(m) * in_dev + first
            if relative:
                at = pl.multiple_of(at, 8)
            per = chans // len(outs)
            block = spec[pl.ds(at, count), :].astype(jnp.bfloat16)
            outs[m // per][m % per, first : first + count, :] = block

    count = in_dev // GROUP
    lax.fori_loop(0, count, step, 0)
    finish(count - 1, True)
    emit(0, in_dev)
    edge[...] = jnp.zeros_like(edge)
    for p in range(2):
        for bank in range(2):
            rows = carry[bank, p * chans : (p + 1) * chans, :]
            edge[pl.ds(2 * p + bank, chans, stride=8), :] = rows
    for m in range(chans):
        per = chans // len(outs)
        at = slot(m) * 8
        if relative:
            at = pl.multiple_of(at, 8)
        count = outs[0].shape[1] - in_dev
        block = edge[pl.ds(at, count), :].astype(jnp.bfloat16)
        outs[m // per][m % per, in_dev:, :] = block


def channelize(samples, chan_index, me, relative, mesh_shape):
    in_dev, fr_dev, frame = samples.shape
    chans = chan_index.shape[0]
    rows = (in_dev + 4 + 7) // 8 * 8
    products = TAPS * 2 * chans
    parts = mesh_shape[0] if relative else 1
    out = jax.ShapeDtypeStruct((chans // parts, rows, LANES), jnp.bfloat16)
    chan_index = pltpu.with_memory_space_constraint(chan_index, pltpu.HBM)
    return pl.pallas_call(
        functools.partial(channelize_kernel, chans, relative, mesh_shape),
        in_specs=[
            pl.BlockSpec(memory_space=pltpu.HBM),
            pl.BlockSpec(memory_space=pltpu.HBM),
        ],
        out_specs=[pl.BlockSpec(memory_space=pltpu.VMEM)] * parts,
        out_shape=[out] * parts,
        scratch_shapes=[
            pltpu.VMEM(samples.shape, jnp.int32),
            pltpu.VMEM((PIECES * products, frame), NARROW),
            pltpu.VMEM((2, products, GROUP * fr_dev), jnp.float32),
            pltpu.VMEM(((chans + 1) * in_dev, LANES), jnp.float32),
            pltpu.VMEM((2, 2 * chans, LANES), jnp.float32),
            pltpu.VMEM(((chans + 1) * 8, LANES), jnp.float32),
            pltpu.SMEM((chans,), jnp.int32),
            pltpu.SemaphoreType.DMA((in_dev // 2,)),
            pltpu.SemaphoreType.DMA,
        ],
        compiler_params=pltpu.CompilerParams(vmem_limit_bytes=48 * 2**20),
        name="channelize",
    )(chan_index, samples)


def place_carry(carried, in_dev, fr_dev):
    mine = lax.broadcasted_iota(jnp.int32, (in_dev, LANES), 0)
    lane = lax.broadcasted_iota(jnp.int32, (in_dev, LANES), 1)
    mask = lane // TAPS == mine // 2 % BANK + (1 - mine % 2) * BANK
    second = mine // 2 >= BANK
    src = lax.broadcasted_iota(jnp.int32, (2 * LANES, LANES), 0)
    dst = lax.broadcasted_iota(jnp.int32, (2 * LANES, LANES), 1)
    place = (src // LANES) * fr_dev + src % TAPS
    spread = jnp.where((place == dst) & (src % TAPS < TAPS - 1), 1.0, 0.0).astype(jnp.bfloat16)
    picked = []
    for four in carried:
        both = []
        for p in range(2):
            row = jnp.where(second, four[2 * p + 1][None], four[2 * p][None])
            both.append(jnp.where(mask, row, 0.0).astype(jnp.bfloat16))
        picked.append(jnp.concatenate(both, axis=1))
    return jnp.dot(
        jnp.concatenate(picked, axis=0), spread, preferred_element_type=jnp.float32
    )


def label(z):
    return z + 0


def place_of(turn):
    at = jnp.int32(0)
    for place, k in enumerate(ORDER):
        at = jnp.where(turn == k, place, at)
    return at


def correlate_kernel(mesh_shape, in_dev, fr_dev, *refs):
    n_freq, n_tm, n_bl = mesh_shape
    own_half, other_half = refs[:n_bl], refs[n_bl : 2 * n_bl]
    o_ref, left, right, result, sems = refs[2 * n_bl :]
    freq, tm, bl = (lax.axis_index(axis) for axis in ("freq", "tm", "bl"))
    scale = 1.0 / (n_tm * fr_dev)
    order = [(f, k) for f in range(n_freq // 2) for k in range(n_bl)]
    for out, base in ((left, bl // 2 * (n_freq // 2)), (right, bl % 2 * (n_freq // 2))):
        early, late, carried, core = [], [], [], []
        for f, k in order:
            at = place_of((label(freq) - label(base + f) + n_freq) % n_freq)
            mine, other = own_half[k], other_half[k]
            core.append(jnp.where(at == 0, 0, 1))
            body, over = slice(0, in_dev), slice(in_dev, in_dev + 4)
            early.append(jnp.where(tm == 0, mine[at, body, :], other[at, body, :]))
            late.append(jnp.where(tm == 0, other[at, body, :], mine[at, body, :]))
            four = jnp.where(tm == 0, mine[at, over, :], other[at, over, :])
            carried.append(four.astype(jnp.float32))
        late = jnp.concatenate(late, axis=0).astype(jnp.float32)
        late = (late + place_carry(carried, in_dev, fr_dev)).astype(jnp.bfloat16)
        for m, (f, k) in enumerate(order):
            at = pl.multiple_of((f * n_bl + (bl ^ k ^ core[m])) * in_dev, in_dev)
            out[pl.ds(at, in_dev), :LANES] = early[m]
            out[pl.ds(at, in_dev), LANES:] = late[m * in_dev : (m + 1) * in_dev]
    half = left.shape[0]
    count = sems.shape[0] // 2
    rows = half // count
    lane = lax.broadcasted_iota(jnp.int32, (rows, LANES), 1)
    dims = (((1,), (1,)), ((), ()))
    copies = []
    for m in range(count):
        span = pl.ds(m * rows, rows)
        mine = left[m * rows : (m + 1) * rows, :]
        turned = []
        for t in range(n_tm):
            part = mine[:, t * LANES : (t + 1) * LANES].astype(jnp.float32)
            part = pltpu.roll(part, fr_dev, 1)
            turned.append(jnp.where(lane < fr_dev, part, -part).astype(jnp.bfloat16))
        for p, a in enumerate((mine, jnp.concatenate(turned, axis=1))):
            result[p, m * rows : (m + 1) * rows, :] = scale * lax.dot_general(
                a, right[...], dims, preferred_element_type=jnp.float32
            )
            copies.append(
                pltpu.make_async_copy(result.at[p, span], o_ref.at[0, 0, p, span], sems.at[2 * m + p])
            )
            copies[-1].start()
    for copy in copies:
        copy.wait()


def correlate(sources, me, mesh_shape, in_dev, fr_dev):
    n_freq, n_tm, n_bl = mesh_shape
    half = n_freq * n_bl * in_dev // 2
    return pl.pallas_call(
        functools.partial(correlate_kernel, mesh_shape, in_dev, fr_dev),
        in_specs=[pl.BlockSpec(memory_space=pltpu.VMEM)] * len(sources),
        out_specs=pl.BlockSpec(memory_space=pl.ANY),
        out_shape=jax.ShapeDtypeStruct((1, 1, 2, half, half), jnp.float32),
        scratch_shapes=[
            pltpu.VMEM((half, n_tm * LANES), jnp.bfloat16),
            pltpu.VMEM((half, n_tm * LANES), jnp.bfloat16),
            pltpu.VMEM((2, half, half), jnp.float32),
            pltpu.SemaphoreType.DMA((4,)),
        ],
        compiler_params=pltpu.CompilerParams(vmem_limit_bytes=16 * 2**20),
        name="correlate",
    )(*sources)


def correlate_plain(gathered, where, n_freq, n_tm, in_dev, fr_dev):
    n_bl = gathered.shape[0]
    half = n_freq * n_bl * in_dev // 2
    blocks = gathered.reshape(n_bl, n_freq, n_tm, -1, LANES)
    blocks = jnp.transpose(blocks, (1, 0, 2, 3, 4)).astype(jnp.float32)
    main = blocks[:, :, :, :in_dev].reshape(n_freq, n_bl, n_tm, in_dev, 2, fr_dev)
    over = blocks[:, :, :-1, in_dev : in_dev + 4]
    over = over.reshape(n_freq, n_bl, n_tm - 1, 2, 2, 2, BANK, TAPS)[:, :, :, :, :, ::-1]
    over = jnp.transpose(over, (0, 1, 2, 4, 6, 5, 3, 7))
    over = over.reshape(n_freq, n_bl, n_tm - 1, 4 * BANK, 2, TAPS)[:, :, :, :in_dev, :, : TAPS - 1]
    over = jnp.pad(over, [(0, 0)] * 2 + [(1, 0)] + [(0, 0)] * 2 + [(0, fr_dev - TAPS + 1)])
    whole = (main + over).astype(jnp.bfloat16)
    whole = jnp.transpose(whole, (4, 0, 1, 3, 2, 5)).reshape(2, 2 * half, n_tm * fr_dev)
    rows = lax.dynamic_slice_in_dim(whole, where[0] * half, half, 1)
    cols = lax.dynamic_slice_in_dim(whole, where[1] * half, half, 1)
    right = jnp.concatenate([cols[0], cols[1]], axis=1)
    left = jnp.stack(
        [jnp.concatenate([rows[0], rows[1]], 1), jnp.concatenate([rows[1], -rows[0]], 1)]
    )
    product = jnp.einsum("phf,qf->phq", left, right, preferred_element_type=jnp.float32)
    return (product / (n_tm * fr_dev))[None, None]


def swapped(block, axes, distance):
    count = math.prod(lax.axis_size(axis) for axis in axes)
    return lax.ppermute(block, axes, [(i, i ^ distance) for i in range(count)])


def exchange(parts, n_tm, n_bl):
    across, plane = ("tm", "bl"), n_tm * n_bl
    arrived = [parts[0]] + [None] * (len(parts) - 1)
    for k in reversed(range(1, len(parts))):
        route = []
        for z in range(len(parts)):
            for i in range(plane):
                to = label((label(z) + k) % len(parts))
                route.append((z * plane + i, to * plane + (i ^ 1)))
        arrived[k] = lax.ppermute(parts[k], ("freq",) + across, route)
    keep = jnp.stack([arrived[k][0] for k in ORDER])
    send = jnp.stack([arrived[k][1] for k in ORDER])
    corner = swapped(send, across, n_bl + 3)
    beside = swapped(send, across, n_bl + 1)
    far = swapped(keep, across, 3)
    turn = lambda block: swapped(block, ("bl",), 1)
    own_half = [keep, turn(keep), turn(far), far]
    other_half = [turn(beside), beside, turn(corner), corner]
    return own_half + other_half


def on_device(samples, chan_index):
    in_dev, fr_dev, frame = samples.shape
    axes = ("freq", "tm", "bl")
    mesh_shape = tuple(lax.axis_size(axis) for axis in axes)
    n_freq, n_tm, n_bl = mesh_shape
    me = lax.axis_index(axes).reshape(1)
    relative = in_dev % 16 == 0 and n_freq <= 4 and n_tm == 2 and n_bl == 4
    spectra = channelize(samples, chan_index, me, relative, mesh_shape)
    if relative:
        sources = exchange(spectra, n_tm, n_bl)
        return correlate(sources, me, mesh_shape, in_dev, fr_dev)
    moved = lax.all_to_all(spectra[0], ("freq", "tm"), split_axis=0, concat_axis=0, tiled=True)
    gathered = lax.all_gather(moved, "bl", axis=0, tiled=False)
    tile = lax.axis_index("bl")
    where = jnp.stack([tile // 2, tile % 2]).astype(jnp.int32)
    return correlate_plain(gathered, where, n_freq, n_tm, in_dev, fr_dev)


def solution(mesh):
    placed = (P(("freq", "bl"), "tm", None), P())
    return jax.shard_map(
        on_device,
        mesh=mesh,
        in_specs=placed,
        out_specs=P(("freq", "tm"), "bl", None, None, None),
        check_vma=False,
    )
```

```python
import functools
import math

import jax
import jax.numpy as jnp
from jax import lax
from jax.experimental import pallas as pl
from jax.experimental.pallas import tpu as pltpu
from jax.sharding import PartitionSpec as P

TAPS = 4
LANES = 128
GROUP = 4
BANK = 16
PIECES = 2
NARROW = jnp.bfloat16
ORDER = (0, 1, 2, 3)


def bin_column(chan_ref, chans):
    row = lax.broadcasted_iota(jnp.int32, (chans, LANES), 0)
    out = jnp.zeros((chans, LANES), jnp.int32)
    for c in range(chans):
        out = jnp.where(row == c, chan_ref[c], out)
    return out[:, :1]


def build_weights(chan_ref, w_ref, chans, frame):
    bins = bin_column(chan_ref, chans)
    steps = lax.broadcasted_iota(jnp.int32, (chans, frame), 1)
    angle = (bins * steps % frame).astype(jnp.float32) * (2.0 * math.pi / frame)
    scale = 1.0 / math.sqrt(frame)
    table = jnp.concatenate([jnp.cos(angle) * scale, -jnp.sin(angle) * scale], axis=0)
    table = table.astype(jnp.bfloat16).astype(jnp.float32) * 0.25
    tap = lax.broadcasted_iota(jnp.int32, (8, frame), 0) % TAPS
    place = lax.broadcasted_iota(jnp.int32, (8, frame), 1) + tap * frame
    place = place.astype(jnp.float32) + 0.5
    turn = math.pi * ((place - 2.0 * frame) / frame)
    window = 0.5 - 0.5 * jnp.cos(place * (2.0 * math.pi / (TAPS * frame)))
    taps = jnp.sin(turn) / turn * window
    left = jnp.concatenate([taps[k : k + 1] * table for k in range(TAPS)], axis=0)
    count = left.shape[0]
    for piece in range(PIECES):
        part = left.astype(NARROW)
        w_ref[piece * count : (piece + 1) * count, :] = part
        left = left - part.astype(jnp.float32)


def shift_and_add(chans, in_dev, fr_dev, pair, part, spec, carry, keep):
    rows = 2 * chans
    lane = lax.broadcasted_iota(jnp.int32, (rows, LANES), 1)
    place = lane % fr_dev
    first = lax.broadcasted_iota(jnp.int32, (chans, LANES), 1) < fr_dev
    own = part[(TAPS - 1) * rows :]
    over = jnp.zeros_like(own)
    for k in range(TAPS - 1):
        late = TAPS - 1 - k
        moved = pltpu.roll(part[k * rows : (k + 1) * rows], late, 1)
        own = own + jnp.where(place >= late, moved, 0.0)
        over = over + jnp.where(place < late, moved, 0.0)
    re, im = own[:chans], own[chans:]
    even = jnp.where(first, re, pltpu.roll(im, fr_dev, 1))
    odd = jnp.where(first, pltpu.roll(re, fr_dev, 1), im)
    spec[pl.ds(pair * 2, chans, stride=in_dev), :] = even
    spec[pl.ds(pair * 2 + 1, chans, stride=in_dev), :] = odd
    over = jnp.where(keep, pltpu.roll(over, pair % BANK * TAPS, 1), 0.0)
    carry[pair // BANK] += over


def channelize_kernel(chans, relative, mesh_shape, chan_hbm, x_ref, *refs):
    outs, refs = refs[: -9], refs[-9:]
    buf, w_ref, raw, spec, carry, edge, chan_ref, sems, chan_sem = refs
    in_dev, fr_dev, frame = x_ref.shape
    n_freq, n_tm, n_bl = mesh_shape
    def fetch(first, count, sem):
        span = pl.ds(first, count)
        return pltpu.make_async_copy(x_ref.at[span], buf.at[span], sems.at[sem])

    chan_copy = pltpu.make_async_copy(chan_hbm, chan_ref, chan_sem)
    chan_copy.start()
    for g in range(in_dev // GROUP):
        fetch(g * GROUP, GROUP, g).start()
    chan_copy.wait()
    build_weights(chan_ref, w_ref, chans, frame)
    carry[...] = jnp.zeros_like(carry)

    def multiply(g):
        fetch(g * GROUP, GROUP, g).wait()
        x = buf[pl.ds(g * GROUP, GROUP)].astype(jnp.float32) - 7.5
        x = x.astype(NARROW).reshape(GROUP * fr_dev, frame)
        pieces = lax.dot_general(
            w_ref[...], x, (((1,), (1,)), ((), ())), preferred_element_type=jnp.float32
        )
        rows = pieces.shape[0] // PIECES
        total = pieces[:rows]
        for piece in range(1, PIECES):
            total += pieces[piece * rows : (piece + 1) * rows]
        return total

    def finish(g, keep):
        for i in range(GROUP // 2):
            part = raw[g % 2, :, i * LANES : (i + 1) * LANES]
            pair = g * (GROUP // 2) + i
            shift_and_add(chans, in_dev, fr_dev, pair, part, spec, carry, keep)

    def step(g, _):
        total = multiply(g)
        finish(jnp.maximum(g - 1, 0), g > 0)
        raw[g % 2] = total
        return 0

    def slot(m):
        if not relative:
            return m
        freq, tm = lax.axis_index("freq"), lax.axis_index("tm")
        return (freq + m // n_tm) % n_freq * n_tm + (tm ^ (m % n_tm))

    def emit(first, count):
        for m in range(chans):
            at = slot(m) * in_dev + first
            if relative:
                at = pl.multiple_of(at, 8)
            per = chans // len(outs)
            block = spec[pl.ds(at, count), :].astype(jnp.bfloat16)
            if relative:
                start = m % per * in_dev + first
                outs[m // per][start : start + count, :] = block
            else:
                outs[0][m, first : first + count, :] = block

    count = in_dev // GROUP
    lax.fori_loop(0, count, step, 0)
    finish(count - 1, True)
    emit(0, in_dev)
    edge[...] = jnp.zeros_like(edge)
    for p in range(2):
        for bank in range(2):
            rows = carry[bank, p * chans : (p + 1) * chans, :]
            edge[pl.ds(2 * p + bank, chans, stride=8), :] = rows
    if relative:
        for k, out in enumerate(outs):
            both = []
            for m in (2 * k, 2 * k + 1):
                both.append(edge[pl.ds(pl.multiple_of(slot(m) * 8, 8), 8), :])
            block = both[0] + pltpu.roll(both[1], 4, 0)
            out[2 * in_dev :, :] = block.astype(jnp.bfloat16)
    else:
        count = outs[0].shape[1] - in_dev
        for m in range(chans):
            block = edge[m * 8 : m * 8 + count, :].astype(jnp.bfloat16)
            outs[0][m, in_dev:, :] = block


def channelize(samples, chan_index, relative, mesh_shape):
    in_dev, fr_dev, frame = samples.shape
    chans = chan_index.shape[0]
    rows = (in_dev + 4 + 7) // 8 * 8
    products = TAPS * 2 * chans
    parts = mesh_shape[0] if relative else 1
    shape = (2 * in_dev + 8, LANES) if relative else (chans, rows, LANES)
    out = jax.ShapeDtypeStruct(shape, jnp.bfloat16)
    chan_index = pltpu.with_memory_space_constraint(chan_index, pltpu.HBM)
    return pl.pallas_call(
        functools.partial(channelize_kernel, chans, relative, mesh_shape),
        in_specs=[
            pl.BlockSpec(memory_space=pltpu.HBM),
            pl.BlockSpec(memory_space=pltpu.HBM),
        ],
        out_specs=[pl.BlockSpec(memory_space=pltpu.VMEM)] * parts,
        out_shape=[out] * parts,
        scratch_shapes=[
            pltpu.VMEM(samples.shape, jnp.int32),
            pltpu.VMEM((PIECES * products, frame), NARROW),
            pltpu.VMEM((2, products, GROUP * fr_dev), jnp.float32),
            pltpu.VMEM(((chans + 1) * in_dev, LANES), jnp.float32),
            pltpu.VMEM((2, 2 * chans, LANES), jnp.float32),
            pltpu.VMEM(((chans + 1) * 8, LANES), jnp.float32),
            pltpu.SMEM((chans,), jnp.int32),
            pltpu.SemaphoreType.DMA((in_dev // 2,)),
            pltpu.SemaphoreType.DMA,
        ],
        compiler_params=pltpu.CompilerParams(vmem_limit_bytes=48 * 2**20),
        name="channelize",
    )(chan_index, samples)


def place_carry(carried, in_dev, fr_dev):
    mine = lax.broadcasted_iota(jnp.int32, (in_dev, LANES), 0)
    lane = lax.broadcasted_iota(jnp.int32, (in_dev, LANES), 1)
    mask = lane // TAPS == mine // 2 % BANK + (1 - mine % 2) * BANK
    second = mine // 2 >= BANK
    src = lax.broadcasted_iota(jnp.int32, (2 * LANES, LANES), 0)
    dst = lax.broadcasted_iota(jnp.int32, (2 * LANES, LANES), 1)
    place = (src // LANES) * fr_dev + src % TAPS
    spread = jnp.where((place == dst) & (src % TAPS < TAPS - 1), 1.0, 0.0).astype(jnp.bfloat16)
    picked = []
    for four in carried:
        both = []
        for p in range(2):
            row = jnp.where(second, four[2 * p + 1], four[2 * p])
            both.append(jnp.where(mask, row, 0.0).astype(jnp.bfloat16))
        picked.append(jnp.concatenate(both, axis=1))
    return jnp.dot(
        jnp.concatenate(picked, axis=0), spread, preferred_element_type=jnp.float32
    )


def place_of(turn):
    at = jnp.int32(0)
    for place, k in enumerate(ORDER):
        at = jnp.where(turn == k, place, at)
    return at


def correlate_kernel(mesh_shape, in_dev, fr_dev, *refs):
    n_freq, n_tm, n_bl = mesh_shape
    own_half, other_half = refs[:n_bl], refs[n_bl : 2 * n_bl]
    o_ref, left, right, result, edges, sems = refs[2 * n_bl :]
    for i in range(2 * n_bl):
        edges[i] = refs[i][n_freq * in_dev :, :].astype(jnp.float32)
    freq, tm, bl = (lax.axis_index(axis) for axis in ("freq", "tm", "bl"))
    scale = 1.0 / (n_tm * fr_dev)
    order = [(f, k) for f in range(n_freq // 2) for k in range(n_bl)]
    for out, base in ((left, bl // 2 * (n_freq // 2)), (right, bl % 2 * (n_freq // 2))):
        early, late, carried, core = [], [], [], []
        for f, k in order:
            at = place_of((freq - base - f + n_freq) % n_freq)
            mine, other = own_half[k], other_half[k]
            core.append(jnp.where(at == 0, 0, 1))
            body = pl.ds(pl.multiple_of(at * in_dev, in_dev), in_dev)
            early.append(jnp.where(tm == 0, mine[body, :], other[body, :]))
            late.append(jnp.where(tm == 0, other[body, :], mine[body, :]))
            giver = jnp.where(tm == 0, k, n_bl + k)
            carried.append([edges[giver, pl.ds(at * 4 + r, 1), :] for r in range(4)])
        late = jnp.concatenate(late, axis=0).astype(jnp.float32)
        late = (late + place_carry(carried, in_dev, fr_dev)).astype(jnp.bfloat16)
        for m, (f, k) in enumerate(order):
            at = pl.multiple_of((f * n_bl + (bl ^ k ^ core[m])) * in_dev, in_dev)
            out[pl.ds(at, in_dev), :LANES] = early[m]
            out[pl.ds(at, in_dev), LANES:] = late[m * in_dev : (m + 1) * in_dev]
    half = left.shape[0]
    count = sems.shape[0] // 2
    rows = half // count
    lane = lax.broadcasted_iota(jnp.int32, (rows, LANES), 1)
    dims = (((1,), (1,)), ((), ()))
    copies = []
    for m in range(count):
        span = pl.ds(m * rows, rows)
        mine = left[m * rows : (m + 1) * rows, :]
        turned = []
        for t in range(n_tm):
            part = mine[:, t * LANES : (t + 1) * LANES].astype(jnp.float32)
            part = pltpu.roll(part, fr_dev, 1)
            turned.append(jnp.where(lane < fr_dev, part, -part).astype(jnp.bfloat16))
        for p, a in enumerate((mine, jnp.concatenate(turned, axis=1))):
            result[p, m * rows : (m + 1) * rows, :] = scale * lax.dot_general(
                a, right[...], dims, preferred_element_type=jnp.float32
            )
            copies.append(
                pltpu.make_async_copy(result.at[p, span], o_ref.at[0, 0, p, span], sems.at[2 * m + p])
            )
            copies[-1].start()
    for copy in copies:
        copy.wait()


def correlate(sources, mesh_shape, in_dev, fr_dev):
    n_freq, n_tm, n_bl = mesh_shape
    half = n_freq * n_bl * in_dev // 2
    return pl.pallas_call(
        functools.partial(correlate_kernel, mesh_shape, in_dev, fr_dev),
        in_specs=[pl.BlockSpec(memory_space=pltpu.VMEM)] * len(sources),
        out_specs=pl.BlockSpec(memory_space=pl.ANY),
        out_shape=jax.ShapeDtypeStruct((1, 1, 2, half, half), jnp.float32),
        scratch_shapes=[
            pltpu.VMEM((half, n_tm * LANES), jnp.bfloat16),
            pltpu.VMEM((half, n_tm * LANES), jnp.bfloat16),
            pltpu.VMEM((2, half, half), jnp.float32),
            pltpu.VMEM((len(sources), 4 * n_freq, LANES), jnp.float32),
            pltpu.SemaphoreType.DMA((4,)),
        ],
        compiler_params=pltpu.CompilerParams(vmem_limit_bytes=16 * 2**20),
        name="correlate",
    )(*sources)


def correlate_plain(gathered, where, n_freq, n_tm, in_dev, fr_dev):
    n_bl = gathered.shape[0]
    half = n_freq * n_bl * in_dev // 2
    blocks = gathered.reshape(n_bl, n_freq, n_tm, -1, LANES)
    blocks = jnp.transpose(blocks, (1, 0, 2, 3, 4)).astype(jnp.float32)
    main = blocks[:, :, :, :in_dev].reshape(n_freq, n_bl, n_tm, in_dev, 2, fr_dev)
    over = blocks[:, :, :-1, in_dev : in_dev + 4]
    over = over.reshape(n_freq, n_bl, n_tm - 1, 2, 2, 2, BANK, TAPS)[:, :, :, :, :, ::-1]
    over = jnp.transpose(over, (0, 1, 2, 4, 6, 5, 3, 7))
    over = over.reshape(n_freq, n_bl, n_tm - 1, 4 * BANK, 2, TAPS)[:, :, :, :in_dev, :, : TAPS - 1]
    over = jnp.pad(over, [(0, 0)] * 2 + [(1, 0)] + [(0, 0)] * 2 + [(0, fr_dev - TAPS + 1)])
    whole = (main + over).astype(jnp.bfloat16)
    whole = jnp.transpose(whole, (4, 0, 1, 3, 2, 5)).reshape(2, 2 * half, n_tm * fr_dev)
    rows = lax.dynamic_slice_in_dim(whole, where[0] * half, half, 1)
    cols = lax.dynamic_slice_in_dim(whole, where[1] * half, half, 1)
    right = jnp.concatenate([cols[0], cols[1]], axis=1)
    left = jnp.stack(
        [jnp.concatenate([rows[0], rows[1]], 1), jnp.concatenate([rows[1], -rows[0]], 1)]
    )
    product = jnp.einsum("phf,qf->phq", left, right, preferred_element_type=jnp.float32)
    return (product / (n_tm * fr_dev))[None, None]


def swapped(block, axes, distance):
    count = math.prod(lax.axis_size(axis) for axis in axes)
    return lax.ppermute(block, axes, [(i, i ^ distance) for i in range(count)])


def exchange(parts, n_tm, n_bl):
    across, plane = ("tm", "bl"), n_tm * n_bl
    arrived = [parts[0]] + [None] * (len(parts) - 1)
    for k in reversed(range(1, len(parts))):
        route = []
        for z in range(len(parts)):
            for i in range(plane):
                to = (z + k) % len(parts)
                route.append((z * plane + i, to * plane + (i ^ 1)))
        arrived[k] = lax.ppermute(parts[k], ("freq",) + across, route)
    rows = [arrived[k] for k in ORDER]
    half = (parts[0].shape[0] - 8) // 2
    keep = [block[:half] for block in rows] + [block[2 * half : 2 * half + 4] for block in rows]
    send = [block[half : 2 * half] for block in rows] + [block[2 * half + 4 :] for block in rows]
    keep, send = jnp.concatenate(keep), jnp.concatenate(send)
    corner = swapped(send, across, n_bl + 3)
    beside = swapped(send, across, n_bl + 1)
    far = swapped(keep, across, 3)
    turn = lambda block: swapped(block, ("bl",), 1)
    own_half = [keep, turn(keep), turn(far), far]
    other_half = [turn(beside), beside, turn(corner), corner]
    return own_half + other_half


def on_device(samples, chan_index):
    in_dev, fr_dev, frame = samples.shape
    axes = ("freq", "tm", "bl")
    mesh_shape = tuple(lax.axis_size(axis) for axis in axes)
    n_freq, n_tm, n_bl = mesh_shape
    relative = in_dev % 16 == 0 and n_freq <= 4 and n_tm == 2 and n_bl == 4
    spectra = channelize(samples, chan_index, relative, mesh_shape)
    if relative:
        sources = exchange(spectra, n_tm, n_bl)
        return correlate(sources, mesh_shape, in_dev, fr_dev)
    moved = lax.all_to_all(spectra[0], ("freq", "tm"), split_axis=0, concat_axis=0, tiled=True)
    gathered = lax.all_gather(moved, "bl", axis=0, tiled=False)
    tile = lax.axis_index("bl")
    where = jnp.stack([tile // 2, tile % 2]).astype(jnp.int32)
    return correlate_plain(gathered, where, n_freq, n_tm, in_dev, fr_dev)


def solution(mesh):
    placed = (P(("freq", "bl"), "tm", None), P())
    return jax.shard_map(
        on_device,
        mesh=mesh,
        in_specs=placed,
        out_specs=P(("freq", "tm"), "bl", None, None, None),
        check_vma=False,
    )
```

```python
import functools
import math

import jax
import jax.numpy as jnp
from jax import lax
from jax.experimental import pallas as pl
from jax.experimental.pallas import tpu as pltpu
from jax.sharding import PartitionSpec as P

TAPS = 4
LANES = 128
GROUP = 4
BANK = 16
PIECES = 2
NARROW = jnp.bfloat16
ORDER = (0, 1, 2, 3)


def bin_column(chan_ref, chans):
    row = lax.broadcasted_iota(jnp.int32, (chans, LANES), 0)
    out = jnp.zeros((chans, LANES), jnp.int32)
    for c in range(chans):
        out = jnp.where(row == c, chan_ref[c], out)
    return out[:, :1]


def build_weights(chan_ref, w_ref, chans, frame):
    bins = bin_column(chan_ref, chans)
    steps = lax.broadcasted_iota(jnp.int32, (chans, frame), 1)
    angle = (bins * steps % frame).astype(jnp.float32) * (2.0 * math.pi / frame)
    scale = 1.0 / math.sqrt(frame)
    table = jnp.concatenate([jnp.cos(angle) * scale, -jnp.sin(angle) * scale], axis=0)
    table = table.astype(jnp.bfloat16).astype(jnp.float32) * 0.25
    tap = lax.broadcasted_iota(jnp.int32, (8, frame), 0) % TAPS
    place = lax.broadcasted_iota(jnp.int32, (8, frame), 1) + tap * frame
    place = place.astype(jnp.float32) + 0.5
    turn = math.pi * ((place - 2.0 * frame) / frame)
    window = 0.5 - 0.5 * jnp.cos(place * (2.0 * math.pi / (TAPS * frame)))
    taps = jnp.sin(turn) / turn * window
    left = jnp.concatenate([taps[k : k + 1] * table for k in range(TAPS)], axis=0)
    count = left.shape[0]
    for piece in range(PIECES):
        part = left.astype(NARROW)
        w_ref[piece * count : (piece + 1) * count, :] = part
        left = left - part.astype(jnp.float32)


def shift_and_add(chans, in_dev, fr_dev, pair, part, spec, carry, keep):
    rows = 2 * chans
    lane = lax.broadcasted_iota(jnp.int32, (rows, LANES), 1)
    place = lane % fr_dev
    first = lax.broadcasted_iota(jnp.int32, (chans, LANES), 1) < fr_dev
    own = part[(TAPS - 1) * rows :]
    over = jnp.zeros_like(own)
    for k in range(TAPS - 1):
        late = TAPS - 1 - k
        moved = pltpu.roll(part[k * rows : (k + 1) * rows], late, 1)
        own = own + jnp.where(place >= late, moved, 0.0)
        over = over + jnp.where(place < late, moved, 0.0)
    re, im = own[:chans], own[chans:]
    even = jnp.where(first, re, pltpu.roll(im, fr_dev, 1))
    odd = jnp.where(first, pltpu.roll(re, fr_dev, 1), im)
    spec[pl.ds(pair * 2, chans, stride=in_dev), :] = even
    spec[pl.ds(pair * 2 + 1, chans, stride=in_dev), :] = odd
    over = jnp.where(keep, pltpu.roll(over, pair % BANK * TAPS, 1), 0.0)
    carry[pair // BANK] += over


def channelize_kernel(chans, relative, mesh_shape, chan_hbm, x_ref, *refs):
    outs, refs = refs[: -9], refs[-9:]
    buf, w_ref, raw, spec, carry, edge, chan_ref, sems, chan_sem = refs
    in_dev, fr_dev, frame = x_ref.shape
    n_freq, n_tm, n_bl = mesh_shape
    def fetch(first, count, sem):
        span = pl.ds(first, count)
        return pltpu.make_async_copy(x_ref.at[span], buf.at[span], sems.at[sem])

    chan_copy = pltpu.make_async_copy(chan_hbm, chan_ref, chan_sem)
    chan_copy.start()
    for g in range(in_dev // GROUP):
        fetch(g * GROUP, GROUP, g).start()
    chan_copy.wait()
    build_weights(chan_ref, w_ref, chans, frame)
    carry[...] = jnp.zeros_like(carry)

    def multiply(g):
        fetch(g * GROUP, GROUP, g).wait()
        x = buf[pl.ds(g * GROUP, GROUP)].astype(jnp.float32) - 7.5
        x = x.astype(NARROW).reshape(GROUP * fr_dev, frame)
        pieces = lax.dot_general(
            w_ref[...], x, (((1,), (1,)), ((), ())), preferred_element_type=jnp.float32
        )
        rows = pieces.shape[0] // PIECES
        total = pieces[:rows]
        for piece in range(1, PIECES):
            total += pieces[piece * rows : (piece + 1) * rows]
        return total

    def finish(g, keep):
        for i in range(GROUP // 2):
            part = raw[g % 2, :, i * LANES : (i + 1) * LANES]
            pair = g * (GROUP // 2) + i
            shift_and_add(chans, in_dev, fr_dev, pair, part, spec, carry, keep)

    def step(g, _):
        total = multiply(g)
        finish(jnp.maximum(g - 1, 0), g > 0)
        raw[g % 2] = total
        return 0

    def slot(m):
        if not relative:
            return m
        freq, tm = lax.axis_index("freq"), lax.axis_index("tm")
        return (freq + m // n_tm) % n_freq * n_tm + (tm ^ (m % n_tm))

    count = in_dev // GROUP
    lax.fori_loop(0, count, step, 0)
    finish(count - 1, True)
    edge[...] = jnp.zeros_like(edge)
    for p in range(2):
        for bank in range(2):
            rows = carry[bank, p * chans : (p + 1) * chans, :]
            edge[pl.ds(2 * p + bank, chans, stride=8), :] = rows
    if relative:
        for k, out in enumerate(outs):
            both = []
            for j in range(2):
                at = slot(2 * k + j)
                own = spec[pl.ds(pl.multiple_of(at * in_dev, in_dev), in_dev), :]
                out[j * in_dev : (j + 1) * in_dev, :] = own.astype(jnp.bfloat16)
                both.append(edge[pl.ds(pl.multiple_of(at * 8, 8), 8), :])
            last = both[0] + pltpu.roll(both[1], 4, 0)
            last = jnp.concatenate([last, jnp.zeros_like(last)], axis=0)
            out[2 * in_dev :, :] = last.astype(jnp.bfloat16)
    else:
        spare = outs[0].shape[1] - in_dev - 4
        for m in range(chans):
            block = [spec[m * in_dev : (m + 1) * in_dev, :], edge[m * 8 : m * 8 + 4, :]]
            if spare:
                block.append(jnp.zeros((spare, LANES), jnp.float32))
            outs[0][m] = jnp.concatenate(block, axis=0).astype(jnp.bfloat16)


def channelize(samples, chan_index, relative, mesh_shape):
    in_dev, fr_dev, frame = samples.shape
    chans = chan_index.shape[0]
    rows = (in_dev + 4 + 15) // 16 * 16
    products = TAPS * 2 * chans
    parts = mesh_shape[0] if relative else 1
    shape = (2 * in_dev + 16, LANES) if relative else (chans, rows, LANES)
    out = jax.ShapeDtypeStruct(shape, jnp.bfloat16)
    chan_index = pltpu.with_memory_space_constraint(chan_index, pltpu.HBM)
    return pl.pallas_call(
        functools.partial(channelize_kernel, chans, relative, mesh_shape),
        in_specs=[
            pl.BlockSpec(memory_space=pltpu.HBM),
            pl.BlockSpec(memory_space=pltpu.HBM),
        ],
        out_specs=[pl.BlockSpec(memory_space=pltpu.VMEM)] * parts,
        out_shape=[out] * parts,
        scratch_shapes=[
            pltpu.VMEM(samples.shape, jnp.int32),
            pltpu.VMEM((PIECES * products, frame), NARROW),
            pltpu.VMEM((2, products, GROUP * fr_dev), jnp.float32),
            pltpu.VMEM(((chans + 1) * in_dev, LANES), jnp.float32),
            pltpu.VMEM((2, 2 * chans, LANES), jnp.float32),
            pltpu.VMEM(((chans + 1) * 8, LANES), jnp.float32),
            pltpu.SMEM((chans,), jnp.int32),
            pltpu.SemaphoreType.DMA((in_dev // 2,)),
            pltpu.SemaphoreType.DMA,
        ],
        compiler_params=pltpu.CompilerParams(vmem_limit_bytes=48 * 2**20),
        name="channelize",
    )(chan_index, samples)


def place_carry(carried, in_dev, fr_dev):
    mine = lax.broadcasted_iota(jnp.int32, (in_dev, LANES), 0)
    lane = lax.broadcasted_iota(jnp.int32, (in_dev, LANES), 1)
    mask = lane // TAPS == mine // 2 % BANK + (1 - mine % 2) * BANK
    second = mine // 2 >= BANK
    src = lax.broadcasted_iota(jnp.int32, (2 * LANES, LANES), 0)
    dst = lax.broadcasted_iota(jnp.int32, (2 * LANES, LANES), 1)
    place = (src // LANES) * fr_dev + src % TAPS
    spread = jnp.where((place == dst) & (src % TAPS < TAPS - 1), 1.0, 0.0).astype(jnp.bfloat16)
    picked = []
    for four in carried:
        both = []
        for p in range(2):
            row = jnp.where(second, four[2 * p + 1], four[2 * p])
            both.append(jnp.where(mask, row, 0.0).astype(jnp.bfloat16))
        picked.append(jnp.concatenate(both, axis=1))
    return jnp.dot(
        jnp.concatenate(picked, axis=0), spread, preferred_element_type=jnp.float32
    )


def place_of(turn):
    at = jnp.int32(0)
    for place, k in enumerate(ORDER):
        at = jnp.where(turn == k, place, at)
    return at


def correlate_kernel(mesh_shape, in_dev, fr_dev, *refs):
    n_freq, n_tm, n_bl = mesh_shape
    own_half, other_half = refs[:n_bl], refs[n_bl : 2 * n_bl]
    o_ref, left, right, result, edges, sems = refs[2 * n_bl :]
    for i in range(2 * n_bl):
        edges[i] = refs[i][n_freq * in_dev :, :].astype(jnp.float32)
    freq, tm, bl = (lax.axis_index(axis) for axis in ("freq", "tm", "bl"))
    scale = 1.0 / (n_tm * fr_dev)
    order = [(f, k) for f in range(n_freq // 2) for k in range(n_bl)]
    for out, base in ((left, bl // 2 * (n_freq // 2)), (right, bl % 2 * (n_freq // 2))):
        early, late, carried, core = [], [], [], []
        for f, k in order:
            at = place_of((freq - base - f + n_freq) % n_freq)
            mine, other = own_half[k], other_half[k]
            core.append(jnp.where(at == 0, 0, 1))
            body = pl.ds(pl.multiple_of(at * in_dev, in_dev), in_dev)
            early.append(jnp.where(tm == 0, mine[body, :], other[body, :]))
            late.append(jnp.where(tm == 0, other[body, :], mine[body, :]))
            giver = jnp.where(tm == 0, k, n_bl + k)
            carried.append([edges[giver, pl.ds(at * 4 + r, 1), :] for r in range(4)])
        late = jnp.concatenate(late, axis=0).astype(jnp.float32)
        late = (late + place_carry(carried, in_dev, fr_dev)).astype(jnp.bfloat16)
        for m, (f, k) in enumerate(order):
            at = pl.multiple_of((f * n_bl + (bl ^ k ^ core[m])) * in_dev, in_dev)
            out[pl.ds(at, in_dev), :LANES] = early[m]
            out[pl.ds(at, in_dev), LANES:] = late[m * in_dev : (m + 1) * in_dev]
    half = left.shape[0]
    count = sems.shape[0] // 2
    rows = half // count
    lane = lax.broadcasted_iota(jnp.int32, (rows, LANES), 1)
    dims = (((1,), (1,)), ((), ()))
    copies = []
    for m in range(count):
        span = pl.ds(m * rows, rows)
        mine = left[m * rows : (m + 1) * rows, :]
        turned = []
        for t in range(n_tm):
            part = mine[:, t * LANES : (t + 1) * LANES].astype(jnp.float32)
            part = pltpu.roll(part, fr_dev, 1)
            turned.append(jnp.where(lane < fr_dev, part, -part).astype(jnp.bfloat16))
        for p, a in enumerate((mine, jnp.concatenate(turned, axis=1))):
            result[p, m * rows : (m + 1) * rows, :] = scale * lax.dot_general(
                a, right[...], dims, preferred_element_type=jnp.float32
            )
            copies.append(
                pltpu.make_async_copy(result.at[p, span], o_ref.at[0, 0, p, span], sems.at[2 * m + p])
            )
            copies[-1].start()
    for copy in copies:
        copy.wait()


def correlate(sources, mesh_shape, in_dev, fr_dev):
    n_freq, n_tm, n_bl = mesh_shape
    half = n_freq * n_bl * in_dev // 2
    return pl.pallas_call(
        functools.partial(correlate_kernel, mesh_shape, in_dev, fr_dev),
        in_specs=[pl.BlockSpec(memory_space=pltpu.VMEM)] * len(sources),
        out_specs=pl.BlockSpec(memory_space=pl.ANY),
        out_shape=jax.ShapeDtypeStruct((1, 1, 2, half, half), jnp.float32),
        scratch_shapes=[
            pltpu.VMEM((half, n_tm * LANES), jnp.bfloat16),
            pltpu.VMEM((half, n_tm * LANES), jnp.bfloat16),
            pltpu.VMEM((2, half, half), jnp.float32),
            pltpu.VMEM((len(sources), 4 * n_freq, LANES), jnp.float32),
            pltpu.SemaphoreType.DMA((4,)),
        ],
        compiler_params=pltpu.CompilerParams(vmem_limit_bytes=16 * 2**20),
        name="correlate",
    )(*sources)


def correlate_plain(gathered, where, n_freq, n_tm, in_dev, fr_dev):
    n_bl = gathered.shape[0]
    half = n_freq * n_bl * in_dev // 2
    blocks = gathered.reshape(n_bl, n_freq, n_tm, -1, LANES)
    blocks = jnp.transpose(blocks, (1, 0, 2, 3, 4)).astype(jnp.float32)
    main = blocks[:, :, :, :in_dev].reshape(n_freq, n_bl, n_tm, in_dev, 2, fr_dev)
    over = blocks[:, :, :-1, in_dev : in_dev + 4]
    over = over.reshape(n_freq, n_bl, n_tm - 1, 2, 2, 2, BANK, TAPS)[:, :, :, :, :, ::-1]
    over = jnp.transpose(over, (0, 1, 2, 4, 6, 5, 3, 7))
    over = over.reshape(n_freq, n_bl, n_tm - 1, 4 * BANK, 2, TAPS)[:, :, :, :in_dev, :, : TAPS - 1]
    over = jnp.pad(over, [(0, 0)] * 2 + [(1, 0)] + [(0, 0)] * 2 + [(0, fr_dev - TAPS + 1)])
    whole = (main + over).astype(jnp.bfloat16)
    whole = jnp.transpose(whole, (4, 0, 1, 3, 2, 5)).reshape(2, 2 * half, n_tm * fr_dev)
    rows = lax.dynamic_slice_in_dim(whole, where[0] * half, half, 1)
    cols = lax.dynamic_slice_in_dim(whole, where[1] * half, half, 1)
    right = jnp.concatenate([cols[0], cols[1]], axis=1)
    left = jnp.stack(
        [jnp.concatenate([rows[0], rows[1]], 1), jnp.concatenate([rows[1], -rows[0]], 1)]
    )
    product = jnp.einsum("phf,qf->phq", left, right, preferred_element_type=jnp.float32)
    return (product / (n_tm * fr_dev))[None, None]


def swapped(block, axes, distance):
    count = math.prod(lax.axis_size(axis) for axis in axes)
    return lax.ppermute(block, axes, [(i, i ^ distance) for i in range(count)])


def exchange(parts, n_tm, n_bl):
    across, plane = ("tm", "bl"), n_tm * n_bl
    arrived = [parts[0]] + [None] * (len(parts) - 1)
    for k in reversed(range(1, len(parts))):
        route = []
        for z in range(len(parts)):
            for i in range(plane):
                to = (z + k) % len(parts)
                route.append((z * plane + i, to * plane + (i ^ 1)))
        arrived[k] = lax.ppermute(parts[k], ("freq",) + across, route)
    rows = [arrived[k] for k in ORDER]
    half = (parts[0].shape[0] - 16) // 2
    keep = [block[:half] for block in rows] + [block[2 * half : 2 * half + 4] for block in rows]
    send = [block[half : 2 * half] for block in rows] + [block[2 * half + 4 : 2 * half + 8] for block in rows]
    keep, send = jnp.concatenate(keep), jnp.concatenate(send)
    corner = swapped(send, across, n_bl + 3)
    beside = swapped(send, across, n_bl + 1)
    far = swapped(keep, across, 3)
    turn = lambda block: swapped(block, ("bl",), 1)
    own_half = [keep, turn(keep), turn(far), far]
    other_half = [turn(beside), beside, turn(corner), corner]
    return own_half + other_half


def on_device(samples, chan_index):
    in_dev, fr_dev, frame = samples.shape
    axes = ("freq", "tm", "bl")
    mesh_shape = tuple(lax.axis_size(axis) for axis in axes)
    n_freq, n_tm, n_bl = mesh_shape
    relative = in_dev % 16 == 0 and n_freq <= 4 and n_tm == 2 and n_bl == 4
    spectra = channelize(samples, chan_index, relative, mesh_shape)
    if relative:
        sources = exchange(spectra, n_tm, n_bl)
        return correlate(sources, mesh_shape, in_dev, fr_dev)
    moved = lax.all_to_all(spectra[0], ("freq", "tm"), split_axis=0, concat_axis=0, tiled=True)
    gathered = lax.all_gather(moved, "bl", axis=0, tiled=False)
    tile = lax.axis_index("bl")
    where = jnp.stack([tile // 2, tile % 2]).astype(jnp.int32)
    return correlate_plain(gathered, where, n_freq, n_tm, in_dev, fr_dev)


def solution(mesh):
    placed = (P(("freq", "bl"), "tm", None), P())
    return jax.shard_map(
        on_device,
        mesh=mesh,
        in_specs=placed,
        out_specs=P(("freq", "tm"), "bl", None, None, None),
        check_vma=False,
    )
```

```python
import functools
import math

import jax
import jax.numpy as jnp
from jax import lax
from jax.experimental import pallas as pl
from jax.experimental.pallas import tpu as pltpu
from jax.sharding import PartitionSpec as P

TAPS = 4
LANES = 128
GROUP = 4
BANK = 16
PIECES = 2
NARROW = jnp.bfloat16
ORDER = (0, 1, 2, 3)


def bin_column(chan_ref, chans):
    row = lax.broadcasted_iota(jnp.int32, (chans, LANES), 0)
    out = jnp.zeros((chans, LANES), jnp.int32)
    for c in range(chans):
        out = jnp.where(row == c, chan_ref[c], out)
    return out[:, :1]


def build_weights(chan_ref, w_ref, chans, frame):
    bins = bin_column(chan_ref, chans)
    steps = lax.broadcasted_iota(jnp.int32, (chans, frame), 1)
    angle = (bins * steps % frame).astype(jnp.float32) * (2.0 * math.pi / frame)
    scale = 1.0 / math.sqrt(frame)
    table = jnp.concatenate([jnp.cos(angle) * scale, -jnp.sin(angle) * scale], axis=0)
    table = table.astype(jnp.bfloat16).astype(jnp.float32) * 0.25
    tap = lax.broadcasted_iota(jnp.int32, (8, frame), 0) % TAPS
    place = lax.broadcasted_iota(jnp.int32, (8, frame), 1) + tap * frame
    place = place.astype(jnp.float32) + 0.5
    turn = math.pi * ((place - 2.0 * frame) / frame)
    window = 0.5 - 0.5 * jnp.cos(place * (2.0 * math.pi / (TAPS * frame)))
    taps = jnp.sin(turn) / turn * window
    left = jnp.concatenate([taps[k : k + 1] * table for k in range(TAPS)], axis=0)
    count = left.shape[0]
    for piece in range(PIECES):
        part = left.astype(NARROW)
        w_ref[piece * count : (piece + 1) * count, :] = part
        left = left - part.astype(jnp.float32)


def shift_and_add(chans, in_dev, fr_dev, pair, part, spec, carry, keep):
    rows = 2 * chans
    lane = lax.broadcasted_iota(jnp.int32, (rows, LANES), 1)
    place = lane % fr_dev
    first = lax.broadcasted_iota(jnp.int32, (chans, LANES), 1) < fr_dev
    own = part[(TAPS - 1) * rows :]
    over = jnp.zeros_like(own)
    for k in range(TAPS - 1):
        late = TAPS - 1 - k
        moved = pltpu.roll(part[k * rows : (k + 1) * rows], late, 1)
        own = own + jnp.where(place >= late, moved, 0.0)
        over = over + jnp.where(place < late, moved, 0.0)
    re, im = own[:chans], own[chans:]
    even = jnp.where(first, re, pltpu.roll(im, fr_dev, 1))
    odd = jnp.where(first, pltpu.roll(re, fr_dev, 1), im)
    spec[pl.ds(pair * 2, chans, stride=in_dev), :] = even
    spec[pl.ds(pair * 2 + 1, chans, stride=in_dev), :] = odd
    over = jnp.where(keep, pltpu.roll(over, pair % BANK * TAPS, 1), 0.0)
    carry[pair // BANK] += over


def channelize_kernel(chans, relative, mesh_shape, chan_hbm, x_ref, *refs):
    outs, refs = refs[: -9], refs[-9:]
    buf, w_ref, raw, spec, carry, edge, chan_ref, sems, chan_sem = refs
    in_dev, fr_dev, frame = x_ref.shape
    n_freq, n_tm, n_bl = mesh_shape
    def fetch(first, count, sem):
        span = pl.ds(first, count)
        return pltpu.make_async_copy(x_ref.at[span], buf.at[span], sems.at[sem])

    chan_copy = pltpu.make_async_copy(chan_hbm, chan_ref, chan_sem)
    chan_copy.start()
    for g in range(in_dev // GROUP):
        fetch(g * GROUP, GROUP, g).start()
    chan_copy.wait()
    build_weights(chan_ref, w_ref, chans, frame)
    carry[...] = jnp.zeros_like(carry)

    def multiply(g):
        fetch(g * GROUP, GROUP, g).wait()
        x = buf[pl.ds(g * GROUP, GROUP)].astype(jnp.float32) - 7.5
        x = x.astype(NARROW).reshape(GROUP * fr_dev, frame)
        pieces = lax.dot_general(
            w_ref[...], x, (((1,), (1,)), ((), ())), preferred_element_type=jnp.float32
        )
        rows = pieces.shape[0] // PIECES
        total = pieces[:rows]
        for piece in range(1, PIECES):
            total += pieces[piece * rows : (piece + 1) * rows]
        return total

    def finish(g, keep):
        for i in range(GROUP // 2):
            part = raw[g % 2, :, i * LANES : (i + 1) * LANES]
            pair = g * (GROUP // 2) + i
            shift_and_add(chans, in_dev, fr_dev, pair, part, spec, carry, keep)

    def step(g, _):
        total = multiply(g)
        finish(jnp.maximum(g - 1, 0), g > 0)
        raw[g % 2] = total
        return 0

    def slot(m):
        if not relative:
            return m
        freq, tm = lax.axis_index("freq"), lax.axis_index("tm")
        return (freq + m // n_tm) % n_freq * n_tm + (tm ^ (m % n_tm))

    count = in_dev // GROUP
    lax.fori_loop(0, count, step, 0)
    finish(count - 1, True)
    edge[...] = jnp.zeros_like(edge)
    for p in range(2):
        for bank in range(2):
            rows = carry[bank, p * chans : (p + 1) * chans, :]
            edge[pl.ds(2 * p + bank, chans, stride=8), :] = rows
    if relative:
        for k, out in enumerate(outs):
            both = []
            for j in range(2):
                at = slot(2 * k + j)
                own = spec[pl.ds(pl.multiple_of(at * in_dev, in_dev), in_dev), :]
                out[j * in_dev : (j + 1) * in_dev, :] = own.astype(jnp.bfloat16)
                both.append(edge[pl.ds(pl.multiple_of(at * 8, 8), 8), :])
            last = both[0] + pltpu.roll(both[1], 4, 0)
            last = jnp.concatenate([last, jnp.zeros_like(last)], axis=0)
            out[2 * in_dev :, :] = last.astype(jnp.bfloat16)
    else:
        spare = outs[0].shape[1] - in_dev - 4
        for m in range(chans):
            block = [spec[m * in_dev : (m + 1) * in_dev, :], edge[m * 8 : m * 8 + 4, :]]
            if spare:
                block.append(jnp.zeros((spare, LANES), jnp.float32))
            outs[0][m] = jnp.concatenate(block, axis=0).astype(jnp.bfloat16)


def channelize(samples, chan_index, relative, mesh_shape):
    in_dev, fr_dev, frame = samples.shape
    chans = chan_index.shape[0]
    rows = (in_dev + 4 + 15) // 16 * 16
    products = TAPS * 2 * chans
    parts = mesh_shape[0] if relative else 1
    shape = (2 * in_dev + 16, LANES) if relative else (chans, rows, LANES)
    out = jax.ShapeDtypeStruct(shape, jnp.bfloat16)
    chan_index = pltpu.with_memory_space_constraint(chan_index, pltpu.HBM)
    return pl.pallas_call(
        functools.partial(channelize_kernel, chans, relative, mesh_shape),
        in_specs=[
            pl.BlockSpec(memory_space=pltpu.HBM),
            pl.BlockSpec(memory_space=pltpu.HBM),
        ],
        out_specs=[pl.BlockSpec(memory_space=pltpu.VMEM)] * parts,
        out_shape=[out] * parts,
        scratch_shapes=[
            pltpu.VMEM(samples.shape, jnp.int32),
            pltpu.VMEM((PIECES * products, frame), NARROW),
            pltpu.VMEM((2, products, GROUP * fr_dev), jnp.float32),
            pltpu.VMEM(((chans + 1) * in_dev, LANES), jnp.float32),
            pltpu.VMEM((2, 2 * chans, LANES), jnp.float32),
            pltpu.VMEM(((chans + 1) * 8, LANES), jnp.float32),
            pltpu.SMEM((chans,), jnp.int32),
            pltpu.SemaphoreType.DMA((in_dev // 2,)),
            pltpu.SemaphoreType.DMA,
        ],
        compiler_params=pltpu.CompilerParams(vmem_limit_bytes=48 * 2**20),
        name="channelize",
    )(chan_index, samples)


def place_carry(carried, in_dev, fr_dev):
    mine = lax.broadcasted_iota(jnp.int32, (in_dev, LANES), 0)
    lane = lax.broadcasted_iota(jnp.int32, (in_dev, LANES), 1)
    mask = lane // TAPS == mine // 2 % BANK + (1 - mine % 2) * BANK
    second = mine // 2 >= BANK
    src = lax.broadcasted_iota(jnp.int32, (2 * LANES, LANES), 0)
    dst = lax.broadcasted_iota(jnp.int32, (2 * LANES, LANES), 1)
    place = (src // LANES) * fr_dev + src % TAPS
    spread = jnp.where((place == dst) & (src % TAPS < TAPS - 1), 1.0, 0.0).astype(jnp.bfloat16)
    picked = []
    for four in carried:
        both = []
        for p in range(2):
            row = jnp.where(second, four[2 * p + 1], four[2 * p])
            both.append(jnp.where(mask, row, 0.0).astype(jnp.bfloat16))
        picked.append(jnp.concatenate(both, axis=1))
    return jnp.dot(
        jnp.concatenate(picked, axis=0), spread, preferred_element_type=jnp.float32
    )


def place_of(turn):
    at = jnp.int32(0)
    for place, k in enumerate(ORDER):
        at = jnp.where(turn == k, place, at)
    return at


def correlate_kernel(mesh_shape, in_dev, fr_dev, *refs):
    n_freq, n_tm, n_bl = mesh_shape
    own_half, other_half = refs[:n_bl], refs[n_bl : 2 * n_bl]
    o_ref, left, right, result, edges, sems = refs[2 * n_bl :]
    for i in range(2 * n_bl):
        edges[i] = refs[i][n_freq * in_dev :, :].astype(jnp.float32)
    freq, tm, bl = (lax.axis_index(axis) for axis in ("freq", "tm", "bl"))
    scale = 1.0 / (n_tm * fr_dev)
    order = [(f, k) for f in range(n_freq // 2) for k in range(n_bl)]
    for out, base in ((left, bl // 2 * (n_freq // 2)), (right, bl % 2 * (n_freq // 2))):
        early, late, carried, core = [], [], [], []
        for f, k in order:
            at = place_of((freq - base - f + n_freq) % n_freq)
            mine, other = own_half[k], other_half[k]
            core.append(jnp.where(at == 0, 0, 1))
            body = pl.ds(pl.multiple_of(at * in_dev, in_dev), in_dev)
            early.append(jnp.where(tm == 0, mine[body, :], other[body, :]))
            late.append(jnp.where(tm == 0, other[body, :], mine[body, :]))
            giver = jnp.where(tm == 0, k, n_bl + k)
            carried.append([edges[giver, pl.ds(at * 4 + r, 1), :] for r in range(4)])
        late = jnp.concatenate(late, axis=0).astype(jnp.float32)
        late = (late + place_carry(carried, in_dev, fr_dev)).astype(jnp.bfloat16)
        for m, (f, k) in enumerate(order):
            at = pl.multiple_of((f * n_bl + (bl ^ k ^ core[m])) * in_dev, in_dev)
            out[pl.ds(at, in_dev), :LANES] = early[m]
            out[pl.ds(at, in_dev), LANES:] = late[m * in_dev : (m + 1) * in_dev]
    half = left.shape[0]
    count = sems.shape[0] // 2
    rows = half // count
    lane = lax.broadcasted_iota(jnp.int32, (rows, LANES), 1)
    dims = (((1,), (1,)), ((), ()))
    copies = []
    for m in range(count):
        span = pl.ds(m * rows, rows)
        mine = left[m * rows : (m + 1) * rows, :]
        turned = []
        for t in range(n_tm):
            part = mine[:, t * LANES : (t + 1) * LANES].astype(jnp.float32)
            part = pltpu.roll(part, fr_dev, 1)
            turned.append(jnp.where(lane < fr_dev, part, -part).astype(jnp.bfloat16))
        for p, a in enumerate((mine, jnp.concatenate(turned, axis=1))):
            result[p, m * rows : (m + 1) * rows, :] = scale * lax.dot_general(
                a, right[...], dims, preferred_element_type=jnp.float32
            )
            copies.append(
                pltpu.make_async_copy(result.at[p, span], o_ref.at[0, 0, p, span], sems.at[2 * m + p])
            )
            copies[-1].start()
    for copy in copies:
        copy.wait()


def correlate(sources, mesh_shape, in_dev, fr_dev):
    n_freq, n_tm, n_bl = mesh_shape
    half = n_freq * n_bl * in_dev // 2
    return pl.pallas_call(
        functools.partial(correlate_kernel, mesh_shape, in_dev, fr_dev),
        in_specs=[pl.BlockSpec(memory_space=pltpu.VMEM)] * len(sources),
        out_specs=pl.BlockSpec(memory_space=pl.ANY),
        out_shape=jax.ShapeDtypeStruct((1, 1, 2, half, half), jnp.float32),
        scratch_shapes=[
            pltpu.VMEM((half, n_tm * LANES), jnp.bfloat16),
            pltpu.VMEM((half, n_tm * LANES), jnp.bfloat16),
            pltpu.VMEM((2, half, half), jnp.float32),
            pltpu.VMEM((len(sources), 4 * n_freq, LANES), jnp.float32),
            pltpu.SemaphoreType.DMA((4,)),
        ],
        compiler_params=pltpu.CompilerParams(vmem_limit_bytes=16 * 2**20),
        name="correlate",
    )(*sources)


def correlate_plain(gathered, where, n_freq, n_tm, in_dev, fr_dev):
    n_bl = gathered.shape[0]
    half = n_freq * n_bl * in_dev // 2
    blocks = gathered.reshape(n_bl, n_freq, n_tm, -1, LANES)
    blocks = jnp.transpose(blocks, (1, 0, 2, 3, 4)).astype(jnp.float32)
    main = blocks[:, :, :, :in_dev].reshape(n_freq, n_bl, n_tm, in_dev, 2, fr_dev)
    over = blocks[:, :, :-1, in_dev : in_dev + 4]
    over = over.reshape(n_freq, n_bl, n_tm - 1, 2, 2, 2, BANK, TAPS)[:, :, :, :, :, ::-1]
    over = jnp.transpose(over, (0, 1, 2, 4, 6, 5, 3, 7))
    over = over.reshape(n_freq, n_bl, n_tm - 1, 4 * BANK, 2, TAPS)[:, :, :, :in_dev, :, : TAPS - 1]
    over = jnp.pad(over, [(0, 0)] * 2 + [(1, 0)] + [(0, 0)] * 2 + [(0, fr_dev - TAPS + 1)])
    whole = (main + over).astype(jnp.bfloat16)
    whole = jnp.transpose(whole, (4, 0, 1, 3, 2, 5)).reshape(2, 2 * half, n_tm * fr_dev)
    rows = lax.dynamic_slice_in_dim(whole, where[0] * half, half, 1)
    cols = lax.dynamic_slice_in_dim(whole, where[1] * half, half, 1)
    right = jnp.concatenate([cols[0], cols[1]], axis=1)
    left = jnp.stack(
        [jnp.concatenate([rows[0], rows[1]], 1), jnp.concatenate([rows[1], -rows[0]], 1)]
    )
    product = jnp.einsum("phf,qf->phq", left, right, preferred_element_type=jnp.float32)
    return (product / (n_tm * fr_dev))[None, None]


def swapped(block, axes, distance):
    count = math.prod(lax.axis_size(axis) for axis in axes)
    return lax.ppermute(block, axes, [(i, i ^ distance) for i in range(count)])


def exchange(parts, n_tm, n_bl):
    across, plane = ("tm", "bl"), n_tm * n_bl
    arrived = [parts[0]] + [None] * (len(parts) - 1)
    for k in reversed(range(1, len(parts))):
        route = []
        for z in range(len(parts)):
            for i in range(plane):
                to = (z + k) % len(parts)
                route.append((z * plane + i, to * plane + (i ^ 1)))
        arrived[k] = lax.ppermute(parts[k], ("freq",) + across, route)
    half = (parts[0].shape[0] - 16) // 2
    count = len(parts)
    keep = jnp.zeros((count * (half + 4), LANES), jnp.bfloat16)
    send = jnp.zeros((count * (half + 4), LANES), jnp.bfloat16)
    for place, k in enumerate(ORDER):
        block, last = arrived[k], count * half + 4 * place
        keep = lax.dynamic_update_slice(keep, block[:half], (place * half, 0))
        keep = lax.dynamic_update_slice(keep, block[2 * half : 2 * half + 4], (last, 0))
        send = lax.dynamic_update_slice(send, block[half : 2 * half], (place * half, 0))
        send = lax.dynamic_update_slice(send, block[2 * half + 4 : 2 * half + 8], (last, 0))
    corner = swapped(send, across, n_bl + 3)
    beside = swapped(send, across, n_bl + 1)
    far = swapped(keep, across, 3)
    turn = lambda block: swapped(block, ("bl",), 1)
    own_half = [keep, turn(keep), turn(far), far]
    other_half = [turn(beside), beside, turn(corner), corner]
    return own_half + other_half


def on_device(samples, chan_index):
    in_dev, fr_dev, frame = samples.shape
    axes = ("freq", "tm", "bl")
    mesh_shape = tuple(lax.axis_size(axis) for axis in axes)
    n_freq, n_tm, n_bl = mesh_shape
    relative = in_dev % 16 == 0 and n_freq <= 4 and n_tm == 2 and n_bl == 4
    spectra = channelize(samples, chan_index, relative, mesh_shape)
    if relative:
        sources = exchange(spectra, n_tm, n_bl)
        return correlate(sources, mesh_shape, in_dev, fr_dev)
    moved = lax.all_to_all(spectra[0], ("freq", "tm"), split_axis=0, concat_axis=0, tiled=True)
    gathered = lax.all_gather(moved, "bl", axis=0, tiled=False)
    tile = lax.axis_index("bl")
    where = jnp.stack([tile // 2, tile % 2]).astype(jnp.int32)
    return correlate_plain(gathered, where, n_freq, n_tm, in_dev, fr_dev)


def solution(mesh):
    placed = (P(("freq", "bl"), "tm", None), P())
    return jax.shard_map(
        on_device,
        mesh=mesh,
        in_specs=placed,
        out_specs=P(("freq", "tm"), "bl", None, None, None),
        check_vma=False,
    )
```

```python
import functools
import math

import jax
import jax.numpy as jnp
from jax import lax
from jax.experimental import pallas as pl
from jax.experimental.pallas import tpu as pltpu
from jax.sharding import PartitionSpec as P

TAPS = 4
LANES = 128
GROUP = 4
BANK = 16
PIECES = 2
NARROW = jnp.bfloat16
ORDER = (0, 1, 2, 3)
SEATS = (5, 4, 7, 6, 3, 2, 0, 1)


def bin_column(chan_ref, chans):
    row = lax.broadcasted_iota(jnp.int32, (chans, LANES), 0)
    out = jnp.zeros((chans, LANES), jnp.int32)
    for c in range(chans):
        out = jnp.where(row == c, chan_ref[c], out)
    return out[:, :1]


def build_weights(chan_ref, w_ref, chans, frame):
    bins = bin_column(chan_ref, chans)
    steps = lax.broadcasted_iota(jnp.int32, (chans, frame), 1)
    angle = (bins * steps % frame).astype(jnp.float32) * (2.0 * math.pi / frame)
    scale = 1.0 / math.sqrt(frame)
    table = jnp.concatenate([jnp.cos(angle) * scale, -jnp.sin(angle) * scale], axis=0)
    table = table.astype(jnp.bfloat16).astype(jnp.float32) * 0.25
    tap = lax.broadcasted_iota(jnp.int32, (8, frame), 0) % TAPS
    place = lax.broadcasted_iota(jnp.int32, (8, frame), 1) + tap * frame
    place = place.astype(jnp.float32) + 0.5
    turn = math.pi * ((place - 2.0 * frame) / frame)
    window = 0.5 - 0.5 * jnp.cos(place * (2.0 * math.pi / (TAPS * frame)))
    taps = jnp.sin(turn) / turn * window
    left = jnp.concatenate([taps[k : k + 1] * table for k in range(TAPS)], axis=0)
    count = left.shape[0]
    for piece in range(PIECES):
        part = left.astype(NARROW)
        w_ref[piece * count : (piece + 1) * count, :] = part
        left = left - part.astype(jnp.float32)


def shift_and_add(chans, in_dev, fr_dev, pair, part, spec, carry, keep):
    rows = 2 * chans
    lane = lax.broadcasted_iota(jnp.int32, (rows, LANES), 1)
    place = lane % fr_dev
    first = lax.broadcasted_iota(jnp.int32, (chans, LANES), 1) < fr_dev
    own = part[(TAPS - 1) * rows :]
    over = jnp.zeros_like(own)
    for k in range(TAPS - 1):
        late = TAPS - 1 - k
        moved = pltpu.roll(part[k * rows : (k + 1) * rows], late, 1)
        own = own + jnp.where(place >= late, moved, 0.0)
        over = over + jnp.where(place < late, moved, 0.0)
    re, im = own[:chans], own[chans:]
    even = jnp.where(first, re, pltpu.roll(im, fr_dev, 1))
    odd = jnp.where(first, pltpu.roll(re, fr_dev, 1), im)
    spec[pl.ds(pair * 2, chans, stride=in_dev), :] = even
    spec[pl.ds(pair * 2 + 1, chans, stride=in_dev), :] = odd
    over = jnp.where(keep, pltpu.roll(over, pair % BANK * TAPS, 1), 0.0)
    carry[pair // BANK] += over


def channelize_kernel(chans, relative, mesh_shape, chan_hbm, x_ref, *refs):
    outs, refs = refs[: -9], refs[-9:]
    buf, w_ref, raw, spec, carry, edge, chan_ref, sems, chan_sem = refs
    in_dev, fr_dev, frame = x_ref.shape
    n_freq, n_tm, n_bl = mesh_shape
    def fetch(first, count, sem):
        span = pl.ds(first, count)
        return pltpu.make_async_copy(x_ref.at[span], buf.at[span], sems.at[sem])

    chan_copy = pltpu.make_async_copy(chan_hbm, chan_ref, chan_sem)
    chan_copy.start()
    for g in range(in_dev // GROUP):
        fetch(g * GROUP, GROUP, g).start()
    chan_copy.wait()
    build_weights(chan_ref, w_ref, chans, frame)
    carry[...] = jnp.zeros_like(carry)

    def multiply(g):
        fetch(g * GROUP, GROUP, g).wait()
        x = buf[pl.ds(g * GROUP, GROUP)].astype(jnp.float32) - 7.5
        x = x.astype(NARROW).reshape(GROUP * fr_dev, frame)
        pieces = lax.dot_general(
            w_ref[...], x, (((1,), (1,)), ((), ())), preferred_element_type=jnp.float32
        )
        rows = pieces.shape[0] // PIECES
        total = pieces[:rows]
        for piece in range(1, PIECES):
            total += pieces[piece * rows : (piece + 1) * rows]
        return total

    def finish(g, keep):
        for i in range(GROUP // 2):
            part = raw[g % 2, :, i * LANES : (i + 1) * LANES]
            pair = g * (GROUP // 2) + i
            shift_and_add(chans, in_dev, fr_dev, pair, part, spec, carry, keep)

    def step(g, _):
        total = multiply(g)
        finish(jnp.maximum(g - 1, 0), g > 0)
        raw[g % 2] = total
        return 0

    def slot(m):
        if not relative:
            return m
        freq, tm = lax.axis_index("freq"), lax.axis_index("tm")
        return (freq + m // n_tm) % n_freq * n_tm + (tm ^ (m % n_tm))

    count = in_dev // GROUP
    lax.fori_loop(0, count, step, 0)
    finish(count - 1, True)
    edge[...] = jnp.zeros_like(edge)
    for p in range(2):
        for bank in range(2):
            rows = carry[bank, p * chans : (p + 1) * chans, :]
            edge[pl.ds(2 * p + bank, chans, stride=8), :] = rows
    if relative:
        for k, out in enumerate(outs):
            both = []
            for j in range(2):
                at = slot(2 * k + j)
                own = spec[pl.ds(pl.multiple_of(at * in_dev, in_dev), in_dev), :]
                out[j * in_dev : (j + 1) * in_dev, :] = own.astype(jnp.bfloat16)
                both.append(edge[pl.ds(pl.multiple_of(at * 8, 8), 8), :])
            last = both[0] + pltpu.roll(both[1], 4, 0)
            last = jnp.concatenate([last, jnp.zeros_like(last)], axis=0)
            out[2 * in_dev :, :] = last.astype(jnp.bfloat16)
    else:
        spare = outs[0].shape[1] - in_dev - 4
        for m in range(chans):
            block = [spec[m * in_dev : (m + 1) * in_dev, :], edge[m * 8 : m * 8 + 4, :]]
            if spare:
                block.append(jnp.zeros((spare, LANES), jnp.float32))
            outs[0][m] = jnp.concatenate(block, axis=0).astype(jnp.bfloat16)


def channelize(samples, chan_index, relative, mesh_shape):
    in_dev, fr_dev, frame = samples.shape
    chans = chan_index.shape[0]
    rows = (in_dev + 4 + 15) // 16 * 16
    products = TAPS * 2 * chans
    parts = mesh_shape[0] if relative else 1
    shape = (2 * in_dev + 16, LANES) if relative else (chans, rows, LANES)
    out = jax.ShapeDtypeStruct(shape, jnp.bfloat16)
    chan_index = pltpu.with_memory_space_constraint(chan_index, pltpu.HBM)
    return pl.pallas_call(
        functools.partial(channelize_kernel, chans, relative, mesh_shape),
        in_specs=[
            pl.BlockSpec(memory_space=pltpu.HBM),
            pl.BlockSpec(memory_space=pltpu.HBM),
        ],
        out_specs=[pl.BlockSpec(memory_space=pltpu.VMEM)] * parts,
        out_shape=[out] * parts,
        scratch_shapes=[
            pltpu.VMEM(samples.shape, jnp.int32),
            pltpu.VMEM((PIECES * products, frame), NARROW),
            pltpu.VMEM((2, products, GROUP * fr_dev), jnp.float32),
            pltpu.VMEM(((chans + 1) * in_dev, LANES), jnp.float32),
            pltpu.VMEM((2, 2 * chans, LANES), jnp.float32),
            pltpu.VMEM(((chans + 1) * 8, LANES), jnp.float32),
            pltpu.SMEM((chans,), jnp.int32),
            pltpu.SemaphoreType.DMA((in_dev // 2,)),
            pltpu.SemaphoreType.DMA,
        ],
        compiler_params=pltpu.CompilerParams(vmem_limit_bytes=48 * 2**20),
        name="channelize",
    )(chan_index, samples)


def place_carry(carried, in_dev, fr_dev):
    mine = lax.broadcasted_iota(jnp.int32, (in_dev, LANES), 0)
    lane = lax.broadcasted_iota(jnp.int32, (in_dev, LANES), 1)
    mask = lane // TAPS == mine // 2 % BANK + (1 - mine % 2) * BANK
    second = mine // 2 >= BANK
    src = lax.broadcasted_iota(jnp.int32, (2 * LANES, LANES), 0)
    dst = lax.broadcasted_iota(jnp.int32, (2 * LANES, LANES), 1)
    place = (src // LANES) * fr_dev + src % TAPS
    spread = jnp.where((place == dst) & (src % TAPS < TAPS - 1), 1.0, 0.0).astype(jnp.bfloat16)
    picked = []
    for four in carried:
        both = []
        for p in range(2):
            row = jnp.where(second, four[2 * p + 1], four[2 * p])
            both.append(jnp.where(mask, row, 0.0).astype(jnp.bfloat16))
        picked.append(jnp.concatenate(both, axis=1))
    return jnp.dot(
        jnp.concatenate(picked, axis=0), spread, preferred_element_type=jnp.float32
    )


def place_of(turn):
    at = jnp.int32(0)
    for place, k in enumerate(ORDER):
        at = jnp.where(turn == k, place, at)
    return at


def correlate_kernel(mesh_shape, in_dev, fr_dev, *refs):
    n_freq, n_tm, n_bl = mesh_shape
    seated = [refs[SEATS.index(i)] for i in range(2 * n_bl)]
    own_half, other_half = seated[:n_bl], seated[n_bl:]
    o_ref, right, result, edges, sems = refs[2 * n_bl :]
    for i in range(2 * n_bl):
        edges[i] = seated[i][n_freq * in_dev :, :].astype(jnp.float32)
    freq, tm, bl = (lax.axis_index(axis) for axis in ("freq", "tm", "bl"))
    scale = 1.0 / (n_tm * fr_dev)
    half, per = right.shape[0], right.shape[0] // (n_freq // 2)

    def gather(f, base):
        at = place_of((freq - base - f + n_freq) % n_freq)
        core = jnp.where(at == 0, 0, 1)
        body = pl.ds(pl.multiple_of(at * in_dev, in_dev), in_dev)
        early, late, carried, places = [], [], [], []
        for k in range(n_bl):
            mine, other = own_half[k], other_half[k]
            early.append(jnp.where(tm == 0, mine[body, :], other[body, :]))
            late.append(jnp.where(tm == 0, other[body, :], mine[body, :]))
            giver = jnp.where(tm == 0, k, n_bl + k)
            carried.append([edges[giver, pl.ds(at * 4 + r, 1), :] for r in range(4)])
            places.append(pl.multiple_of(f * per + (bl ^ k ^ core) * in_dev, in_dev))
        late = jnp.concatenate(late, axis=0).astype(jnp.float32)
        late = (late + place_carry(carried, in_dev, fr_dev)).astype(jnp.bfloat16)
        return jnp.concatenate(early, axis=0), late, places

    for f in range(n_freq // 2):
        early, late, places = gather(f, bl % 2 * (n_freq // 2))
        for k, at in enumerate(places):
            right[pl.ds(at, in_dev), :LANES] = early[k * in_dev : (k + 1) * in_dev]
            right[pl.ds(at, in_dev), LANES:] = late[k * in_dev : (k + 1) * in_dev]
    lane = lax.broadcasted_iota(jnp.int32, (per, LANES), 1)
    dims = (((1,), (1,)), ((), ()))
    copies = []
    for f in range(n_freq // 2):
        early, late, places = gather(f, bl // 2 * (n_freq // 2))
        turned = []
        for part in (early, late):
            part = pltpu.roll(part.astype(jnp.float32), fr_dev, 1)
            turned.append(jnp.where(lane < fr_dev, part, -part).astype(jnp.bfloat16))
        for p, a in enumerate(((early, late), turned)):
            product = scale * lax.dot_general(
                jnp.concatenate(a, axis=1), right[...], dims, preferred_element_type=jnp.float32
            )
            for k, at in enumerate(places):
                result[p, pl.ds(at, in_dev), :] = product[k * in_dev : (k + 1) * in_dev]
            span = pl.ds(f * per, per)
            copies.append(
                pltpu.make_async_copy(
                    result.at[p, span], o_ref.at[0, 0, p, span], sems.at[2 * f + p]
                )
            )
            copies[-1].start()
    for copy in copies:
        copy.wait()


def correlate(sources, mesh_shape, in_dev, fr_dev):
    n_freq, n_tm, n_bl = mesh_shape
    half = n_freq * n_bl * in_dev // 2
    return pl.pallas_call(
        functools.partial(correlate_kernel, mesh_shape, in_dev, fr_dev),
        in_specs=[pl.BlockSpec(memory_space=pltpu.VMEM)] * len(sources),
        out_specs=pl.BlockSpec(memory_space=pl.ANY),
        out_shape=jax.ShapeDtypeStruct((1, 1, 2, half, half), jnp.float32),
        scratch_shapes=[
            pltpu.VMEM((half, n_tm * LANES), jnp.bfloat16),
            pltpu.VMEM((2, half, half), jnp.float32),
            pltpu.VMEM((len(sources), 4 * n_freq, LANES), jnp.float32),
            pltpu.SemaphoreType.DMA((n_freq,)),
        ],
        compiler_params=pltpu.CompilerParams(vmem_limit_bytes=16 * 2**20),
        name="correlate",
    )(*sources)


def correlate_plain(gathered, where, n_freq, n_tm, in_dev, fr_dev):
    n_bl = gathered.shape[0]
    half = n_freq * n_bl * in_dev // 2
    blocks = gathered.reshape(n_bl, n_freq, n_tm, -1, LANES)
    blocks = jnp.transpose(blocks, (1, 0, 2, 3, 4)).astype(jnp.float32)
    main = blocks[:, :, :, :in_dev].reshape(n_freq, n_bl, n_tm, in_dev, 2, fr_dev)
    over = blocks[:, :, :-1, in_dev : in_dev + 4]
    over = over.reshape(n_freq, n_bl, n_tm - 1, 2, 2, 2, BANK, TAPS)[:, :, :, :, :, ::-1]
    over = jnp.transpose(over, (0, 1, 2, 4, 6, 5, 3, 7))
    over = over.reshape(n_freq, n_bl, n_tm - 1, 4 * BANK, 2, TAPS)[:, :, :, :in_dev, :, : TAPS - 1]
    over = jnp.pad(over, [(0, 0)] * 2 + [(1, 0)] + [(0, 0)] * 2 + [(0, fr_dev - TAPS + 1)])
    whole = (main + over).astype(jnp.bfloat16)
    whole = jnp.transpose(whole, (4, 0, 1, 3, 2, 5)).reshape(2, 2 * half, n_tm * fr_dev)
    rows = lax.dynamic_slice_in_dim(whole, where[0] * half, half, 1)
    cols = lax.dynamic_slice_in_dim(whole, where[1] * half, half, 1)
    right = jnp.concatenate([cols[0], cols[1]], axis=1)
    left = jnp.stack(
        [jnp.concatenate([rows[0], rows[1]], 1), jnp.concatenate([rows[1], -rows[0]], 1)]
    )
    product = jnp.einsum("phf,qf->phq", left, right, preferred_element_type=jnp.float32)
    return (product / (n_tm * fr_dev))[None, None]


def swapped(block, axes, distance):
    count = math.prod(lax.axis_size(axis) for axis in axes)
    return lax.ppermute(block, axes, [(i, i ^ distance) for i in range(count)])


def exchange(parts, n_tm, n_bl):
    across, plane = ("tm", "bl"), n_tm * n_bl
    arrived = [parts[0]] + [None] * (len(parts) - 1)
    for k in reversed(range(1, len(parts))):
        route = []
        for z in range(len(parts)):
            for i in range(plane):
                to = (z + k) % len(parts)
                route.append((z * plane + i, to * plane + (i ^ 1)))
        arrived[k] = lax.ppermute(parts[k], ("freq",) + across, route)
    half = (parts[0].shape[0] - 16) // 2
    count = len(parts)
    keep = jnp.zeros((count * (half + 4), LANES), jnp.bfloat16)
    send = jnp.zeros((count * (half + 4), LANES), jnp.bfloat16)
    for place, k in enumerate(ORDER):
        block, last = arrived[k], count * half + 4 * place
        keep = lax.dynamic_update_slice(keep, block[:half], (place * half, 0))
        keep = lax.dynamic_update_slice(keep, block[2 * half : 2 * half + 4], (last, 0))
        send = lax.dynamic_update_slice(send, block[half : 2 * half], (place * half, 0))
        send = lax.dynamic_update_slice(send, block[2 * half + 4 : 2 * half + 8], (last, 0))
    corner = swapped(send, across, n_bl + 3)
    beside = swapped(send, across, n_bl + 1)
    far = swapped(keep, across, 3)
    turn = lambda block: swapped(block, ("bl",), 1)
    own_half = [keep, turn(keep), turn(far), far]
    other_half = [turn(beside), beside, turn(corner), corner]
    both = own_half + other_half
    return [both[i] for i in SEATS]


def on_device(samples, chan_index):
    in_dev, fr_dev, frame = samples.shape
    axes = ("freq", "tm", "bl")
    mesh_shape = tuple(lax.axis_size(axis) for axis in axes)
    n_freq, n_tm, n_bl = mesh_shape
    relative = in_dev % 16 == 0 and n_freq <= 4 and n_tm == 2 and n_bl == 4
    spectra = channelize(samples, chan_index, relative, mesh_shape)
    if relative:
        sources = exchange(spectra, n_tm, n_bl)
        return correlate(sources, mesh_shape, in_dev, fr_dev)
    moved = lax.all_to_all(spectra[0], ("freq", "tm"), split_axis=0, concat_axis=0, tiled=True)
    gathered = lax.all_gather(moved, "bl", axis=0, tiled=False)
    tile = lax.axis_index("bl")
    where = jnp.stack([tile // 2, tile % 2]).astype(jnp.int32)
    return correlate_plain(gathered, where, n_freq, n_tm, in_dev, fr_dev)


def solution(mesh):
    placed = (P(("freq", "bl"), "tm", None), P())
    return jax.shard_map(
        on_device,
        mesh=mesh,
        in_specs=placed,
        out_specs=P(("freq", "tm"), "bl", None, None, None),
        check_vma=False,
    )
```
